32 devices in a mesh: seq: 4 (over y, x), chan: 8 (over z, core).
Axes of the slice: x: 2, y: 2, z: 4, core: 2. Of those that a mesh axis runs over, the one named last changes fastest.
Arguments:
- hidden: bfloat16 [256, 4096], P('seq', 'chan'), may hold values from -6 to 6
- filters: bfloat16 [256, 4096], P('seq', 'chan'), may hold values from -0.75 to 0.75
- in_weight: bfloat16 [3, 4096, 4096], P(None, None, 'chan'), may hold values from -0.09375 to 0.09375
- out_weight: bfloat16 [4096, 4096], P('chan'), may hold values from -0.125 to 0.125
- block_table: int32 [8], replicated, may hold values from 0 to 7, as said below
Outputs:
- mixed: bfloat16 [256, 4096], P('seq', 'chan')
The draws below stay inside these ranges and needn't reach their ends.
Inputs may be any that keep to these rules, and one draw needn't show every extreme that they name: `block_table`: each index of seq holds stored blocks 2g and 2g+1, which carry a pair p and 7 - p in either order; every sequence block appears once.
All inputs are finite; a program needn't handle non-finite values.
Results may differ from the reference program's by a relative error of at most 0.0049.
Values may be sent and summed in bfloat16 or wider, within the bound.
A program may use at most 64 MiB of HBM per device.

```python
import jax
import jax.numpy as jnp

D = 4096
SEG = 32
BLOCKS = 8
LENGTH = 256
N_SEQ = 4


def draw_block_table(key, part):
    key = jax.random.fold_in(key, 5)
    first_key, second_key = jax.random.split(key)
    pairs = jax.random.permutation(first_key, N_SEQ).astype(jnp.int32)
    flipped = jax.random.randint(second_key, (N_SEQ,), 0, 2)
    late = 2 * N_SEQ - 1 - pairs
    first = jnp.where(flipped == 1, late, pairs)
    second = jnp.where(flipped == 1, pairs, late)
    return jnp.stack([first, second], axis=1).reshape(-1).astype(jnp.int32)


def with_spikes(entries, own_key, source, target, parts, factor):
    def block_of(axis_at):
        return (jnp.arange(entries.shape[axis_at]) // (entries.shape[axis_at] // parts)).reshape((-1,) + (1,) * (entries.ndim - 1 - axis_at))

    first = jax.random.permutation(own_key, parts)[block_of(target)]
    other_side = (block_of(target) + parts // 2) % parts
    return jnp.where((block_of(source) == first) | (block_of(source) == other_side), factor * entries, entries)


def level_of(key, extent, pieces, least, largest):
    factor_of = 1.0
    for position, blocks in pieces:
        heights = jax.random.uniform(jax.random.fold_in(jax.random.fold_in(key, 6), position), (blocks,), jnp.float32, least / len(pieces), largest / len(pieces))
        factor_of = factor_of * jnp.repeat(jnp.exp(heights), extent[position] // blocks).reshape((-1,) + (1,) * (len(extent) - 1 - position))
    return factor_of


def noise(key, extent, width, bound, shards=(), kind=jnp.bfloat16):
    factor_of = level_of(key, extent, shards, -0.22, 0.18) if shards else 1.0
    values = jax.random.normal(key, extent, jnp.float32) * width * factor_of
    return jnp.minimum(jnp.maximum(values, -bound), bound).astype(kind)


def noise_with(stream_key, shape, deviation, bound, cuts, heavy, kind=jnp.bfloat16):
    values = deviation * jax.random.normal(stream_key, shape, jnp.float32)
    if cuts:
        values = values * level_of(stream_key, shape, cuts, -0.22, 0.18)
    return jnp.clip(with_spikes(values, jax.random.fold_in(stream_key, 3), *heavy), -bound, bound).astype(kind)


def setup_inputs(seed: int = 0) -> dict:
    seeds = jax.random.split(jax.random.key(seed), 6)
    return {
        "hidden": noise(seeds[0], (LENGTH, D), 1.0, 6.0, ((0, 4), (1, 8))),
        "filters": noise(seeds[1], (LENGTH, D), (2.0 / LENGTH ** 0.5), 0.75, ((0, 4), (1, 8))),
        "in_weight": noise(seeds[2], (3, D, D), D ** -0.5, 0.09375, ((2, 8),)),
        "out_weight": noise_with(seeds[3], (D, D), D ** -0.5, 0.125, ((0, 8),), (0, 1, 8, 2.0)),
        "block_table": draw_block_table(jax.random.fold_in(seeds[5], 71), 0),
    }


def reference(hidden, filters, in_weight, out_weight, block_table):
    order = jnp.zeros((BLOCKS,), jnp.int32).at[block_table].set(jnp.arange(BLOCKS, dtype=jnp.int32))
    ordered = hidden.reshape(BLOCKS, SEG, D)[order].reshape(LENGTH, D)
    query = jnp.dot(ordered, in_weight[0], preferred_element_type=jnp.float32)
    keys = jnp.dot(ordered, in_weight[1], preferred_element_type=jnp.float32)
    values = jnp.dot(ordered, in_weight[2], preferred_element_type=jnp.float32)
    mixed_in = keys * values
    kernel = filters.astype(jnp.float32)
    total = 2 * LENGTH
    conv = jnp.fft.irfft(jnp.fft.rfft(mixed_in, total, axis=0) * jnp.fft.rfft(kernel, total, axis=0), total, axis=0)[:LENGTH]
    gated = (query * conv).astype(jnp.bfloat16)
    projected = jnp.dot(gated, out_weight, preferred_element_type=jnp.float32).astype(jnp.bfloat16)
    return projected.reshape(BLOCKS, SEG, D)[block_table].reshape(LENGTH, D)
```

```python
import functools

import jax
import jax.numpy as jnp
from jax import lax
from jax.experimental import pallas as pl
from jax.experimental.pallas import tpu as pltpu
from jax.sharding import PartitionSpec as P

MESH = pl.DeviceIdType.MESH
LANES = 128


def flip(value, bits):
    result, bit = value, 1
    while bit <= bits:
        if bits & bit:
            result = result + bit - 2 * bit * ((value // bit) % 2)
        bit *= 2
    return result


def kernel(
    n_seq,
    n_chan,
    hidden_ref,
    filters_ref,
    win_ref,
    wout_ref,
    table_ref,
    out_ref,
    hbuf,
    fbuf,
    win,
    wout,
    streams,
    fpad,
    msend,
    mrecv,
    mwork,
    acc,
    gated,
    psend,
    precv,
    ssend,
    srecv,
    own_sem,
    win_sem,
    wout_sem,
    hz_send,
    hz_recv,
    hp_send,
    hp_recv,
    f_send,
    f_recv,
    m_send,
    m_recv,
    p_send,
    p_recv,
    s_send,
    s_recv,
):
    rows, chans = hidden_ref.shape
    seg = rows // 2
    tiles = seg // 8
    groups = chans // LANES
    n_z = n_chan // 2
    seq = lax.axis_index("seq")
    chan = lax.axis_index("chan")
    z = chan // 2
    core = chan % 2
    partner = 2 * z + 1 - core

    def chan_of(dz):
        return 2 * flip(z, dz) + core

    def lanes_of(which):
        return pl.ds(pl.multiple_of(which * chans, chans), chans)

    def remote(src, dst, send_sem, recv_sem, **where):
        return pltpu.make_async_remote_copy(
            src_ref=src,
            dst_ref=dst,
            send_sem=send_sem,
            recv_sem=recv_sem,
            device_id=where,
            device_id_type=MESH,
        )

    own_hidden = pltpu.make_async_copy(hidden_ref, hbuf.at[z, :, lanes_of(core)], own_sem.at[0])
    own_filters = pltpu.make_async_copy(filters_ref, fbuf.at[seq], own_sem.at[1])
    own_hidden.start()
    own_filters.start()
    win_copies = []
    for dz in range(n_z):
        part = pl.ds(pl.multiple_of(flip(z, dz) * 2 * chans, 2 * chans), 2 * chans)
        copy = pltpu.make_async_copy(win_ref.at[:, part, :], win.at[:, part, :], win_sem.at[dz])
        copy.start()
        win_copies.append(copy)
    wout_copy = pltpu.make_async_copy(wout_ref, wout, wout_sem)
    wout_copy.start()

    barrier = pltpu.get_barrier_semaphore()
    for ds in range(1, n_seq):
        pl.semaphore_signal(barrier, inc=1, device_id={"seq": flip(seq, ds)}, device_id_type=MESH)
    for dz in range(1, n_z):
        pl.semaphore_signal(barrier, inc=1, device_id={"chan": chan_of(dz)}, device_id_type=MESH)
    pl.semaphore_signal(barrier, inc=1, device_id={"chan": partner}, device_id_type=MESH)
    pl.semaphore_wait(barrier, n_seq - 1 + n_z)

    pending = []
    to_chip = {}
    for dz in range(n_z - 1, 0, -1):
        copy = remote(
            hidden_ref, hbuf.at[z, :, lanes_of(core)], hz_send.at[dz - 1], hz_recv.at[dz - 1], chan=chan_of(dz)
        )
        copy.start()
        to_chip[dz] = copy
        pending.append(copy)
    to_partner = {}
    to_partner[0] = remote(
        hidden_ref, hbuf.at[z, :, lanes_of(core)], hp_send.at[0], hp_recv.at[0], chan=partner
    )
    to_partner[0].start()
    pending.append(to_partner[0])
    filter_copies = []
    for ds in range(1, n_seq):
        copy = remote(filters_ref, fbuf.at[seq], f_send.at[ds - 1], f_recv.at[ds - 1], seq=flip(seq, ds))
        copy.start()
        filter_copies.append(copy)
        pending.append(copy)

    def project(dz, which):
        chip = flip(z, dz)
        part = pl.ds(pl.multiple_of(chip * 2 * chans, 2 * chans), 2 * chans)
        total = jnp.dot(hbuf[chip], win[which, part, :], preferred_element_type=jnp.float32)
        if dz == 0:
            streams[which] = total
        else:
            streams[which] += total

    def unpack_filters():
        own_filters.wait()
        for copy in filter_copies:
            copy.wait_recv()
        for group in range(groups):
            lanes = slice(group * LANES, (group + 1) * LANES)
            fpad[group, 0:seg, :] = jnp.zeros((seg, LANES), jnp.float32)
            for piece in range(n_seq):
                fpad[group, seg + piece * rows : seg + (piece + 1) * rows, :] = fbuf[piece, :, lanes].astype(
                    jnp.float32
                )

    own_hidden.wait()
    for dz in range(n_z):
        if dz:
            chip = flip(z, dz)
            to_chip[dz].wait_recv()
            spot = hbuf.at[chip, :, lanes_of(core)]
            to_partner[dz] = remote(spot, spot, hp_send.at[dz], hp_recv.at[dz], chan=partner)
            to_partner[dz].start()
            pending.append(to_partner[dz])
        if dz == n_z - 1:
            unpack_filters()
        to_partner[dz].wait_recv()
        win_copies[dz].wait()
        project(dz, 1)
        project(dz, 2)
        if dz < n_z - 1:
            project(dz, 0)

    first = table_ref[2 * seq]
    second = table_ref[2 * seq + 1]
    early = jnp.minimum(first, second)
    in_order = jnp.full((seg, LANES), first) < jnp.full((seg, LANES), second)
    for group in range(groups):
        lanes = slice(group * LANES, (group + 1) * LANES)
        product = streams[1, :, lanes] * streams[2, :, lanes]
        lead = jnp.where(in_order, product[:seg], product[seg:])
        tail = jnp.where(in_order, product[seg:], product[:seg])
        mwork[0, group] = lead
        mwork[1, group] = tail
        msend[0:seg, lanes] = lead.astype(jnp.bfloat16)
        msend[seg : 2 * seg, lanes] = tail.astype(jnp.bfloat16)
    m_copies = []
    for ds in range(1, n_seq):
        copy = remote(msend, mrecv.at[ds - 1], m_send.at[ds - 1], m_recv.at[ds - 1], seq=flip(seq, ds))
        copy.start()
        m_copies.append(copy)
        pending.append(copy)
    project(n_z - 1, 0)

    def convolve(totals, group, slot, lag, lower=False):
        base = lag * seg + seg
        totals = list(totals)
        for shift in range(8):
            window = {}
            for gap in range(0 if lower else 1 - tiles, tiles):
                window[gap] = fpad[group, pl.ds(base + (8 * gap - shift), 8), :]
            for b in range(tiles):
                row = 8 * b + shift
                value = jnp.broadcast_to(mwork[slot, group, row : row + 1, :], (8, LANES))
                for a in range(b if lower else 0, tiles):
                    totals[a] = totals[a] + window[a - b] * value
        return totals

    def zeros():
        return [jnp.zeros((8, LANES), jnp.float32) for _ in range(tiles)]

    count = 2 * n_seq

    def own_blocks(group, carry):
        lead = convolve(zeros(), group, 0, 0, lower=True)
        tail = convolve(zeros(), group, 1, 0, lower=True)
        tail = convolve(tail, group, 0, count - 1 - 2 * early)
        for a in range(tiles):
            acc[0, group, 8 * a : 8 * a + 8, :] = lead[a]
            acc[1, group, 8 * a : 8 * a + 8, :] = tail[a]
        return carry

    lax.fori_loop(0, groups, own_blocks, 0)

    for ds in range(1, n_seq):
        other = flip(seq, ds)
        theirs = jnp.minimum(table_ref[2 * other], table_ref[2 * other + 1])
        m_copies[ds - 1].wait_recv()
        later = jnp.full((seg, LANES), early) > jnp.full((seg, LANES), theirs)
        later_tile = jnp.full((8, LANES), early) > jnp.full((8, LANES), theirs)
        for group in range(groups):
            lanes = slice(group * LANES, (group + 1) * LANES)
            lead = mrecv[ds - 1, 0:seg, lanes].astype(jnp.float32)
            tail = mrecv[ds - 1, seg : 2 * seg, lanes].astype(jnp.float32)
            mwork[0, group] = lead
            mwork[1, group] = jnp.where(later, lead, tail)

        def other_blocks(group, carry):
            tail = [acc[1, group, 8 * a : 8 * a + 8, :] for a in range(tiles)]
            tail = convolve(tail, group, 0, count - 1 - early - theirs)
            mixed = convolve(zeros(), group, 1, jnp.maximum(early, theirs) - jnp.minimum(early, theirs))
            for a in range(tiles):
                place = slice(8 * a, 8 * a + 8)
                acc[0, group, place, :] += jnp.where(later_tile, mixed[a], 0.0)
                acc[1, group, place, :] = tail[a] + jnp.where(later_tile, 0.0, mixed[a])
            return carry

        lax.fori_loop(0, groups, other_blocks, 0)

    for group in range(groups):
        lanes = slice(group * LANES, (group + 1) * LANES)
        lead = acc[0, group]
        tail = acc[1, group]
        gated[0:seg, lanes] = (streams[0, 0:seg, lanes] * jnp.where(in_order, lead, tail)).astype(jnp.bfloat16)
        gated[seg : 2 * seg, lanes] = (
            streams[0, seg : 2 * seg, lanes] * jnp.where(in_order, tail, lead)
        ).astype(jnp.bfloat16)

    wout_copy.wait()
    order = list(range(n_z - 1, -1, -1))
    p_copies = {}
    for dz in order:
        columns = lanes_of(2 * flip(z, dz) + 1 - core)
        psend[dz] = jnp.dot(gated[...], wout[:, columns], preferred_element_type=jnp.float32).astype(
            jnp.bfloat16
        )
        p_copies[dz] = remote(psend.at[dz], precv.at[dz], p_send.at[dz], p_recv.at[dz], chan=partner)
        p_copies[dz].start()
        pending.append(p_copies[dz])
    s_copies = []
    for dz in order:
        columns = lanes_of(chan_of(dz))
        share = jnp.dot(gated[...], wout[:, columns], preferred_element_type=jnp.float32)
        p_copies[dz].wait_recv()
        share = share + precv[dz].astype(jnp.float32)
        if dz:
            ssend[dz - 1] = share.astype(jnp.bfloat16)
            copy = remote(
                ssend.at[dz - 1], srecv.at[dz - 1], s_send.at[dz - 1], s_recv.at[dz - 1], chan=chan_of(dz)
            )
            copy.start()
            s_copies.append(copy)
            pending.append(copy)
        else:
            streams[0] = share
    for copy in s_copies:
        copy.wait_recv()
    total = streams[0]
    for dz in range(1, n_z):
        total = total + srecv[dz - 1].astype(jnp.float32)
    out_ref[...] = total.astype(jnp.bfloat16)
    for copy in pending:
        copy.wait_send()


def on_device(n_seq, n_chan, hidden, filters, in_weight, out_weight, block_table):
    rows, chans = hidden.shape
    seg = rows // 2
    groups = chans // LANES
    n_z = n_chan // 2
    width = in_weight.shape[1]
    bf16, f32 = jnp.bfloat16, jnp.float32
    dma = pltpu.SemaphoreType.DMA
    anywhere = pl.BlockSpec(memory_space=pl.ANY)
    return pl.pallas_call(
        functools.partial(kernel, n_seq, n_chan),
        out_shape=jax.ShapeDtypeStruct((rows, chans), bf16),
        in_specs=[anywhere] * 4 + [pl.BlockSpec(memory_space=pltpu.SMEM)],
        out_specs=pl.BlockSpec(memory_space=pltpu.VMEM),
        scratch_shapes=[
            pltpu.VMEM((n_z, rows, 2 * chans), bf16),
            pltpu.VMEM((n_seq, rows, chans), bf16),
            pltpu.VMEM((3, width, chans), bf16),
            pltpu.VMEM((chans, width), bf16),
            pltpu.VMEM((3, rows, chans), f32),
            pltpu.VMEM((groups, seg + n_seq * rows, LANES), f32),
            pltpu.VMEM((rows, chans), bf16),
            pltpu.VMEM((n_seq - 1, rows, chans), bf16),
            pltpu.VMEM((2, groups, seg, LANES), f32),
            pltpu.VMEM((2, groups, seg, LANES), f32),
            pltpu.VMEM((rows, chans), bf16),
            pltpu.VMEM((n_z, rows, chans), bf16),
            pltpu.VMEM((n_z, rows, chans), bf16),
            pltpu.VMEM((n_z - 1, rows, chans), bf16),
            pltpu.VMEM((n_z - 1, rows, chans), bf16),
            dma((2,)),
            dma((n_z,)),
            dma,
            dma((n_z - 1,)),
            dma((n_z - 1,)),
            dma((n_z,)),
            dma((n_z,)),
            dma((n_seq - 1,)),
            dma((n_seq - 1,)),
            dma((n_seq - 1,)),
            dma((n_seq - 1,)),
            dma((n_z,)),
            dma((n_z,)),
            dma((n_z - 1,)),
            dma((n_z - 1,)),
        ],
        compiler_params=pltpu.CompilerParams(
            collective_id=0, has_side_effects=True, vmem_limit_bytes=40 * 1024 * 1024
        ),
        cost_estimate=pl.CostEstimate(
            flops=8 * rows * width * chans, bytes_accessed=8 * width * chans, transcendentals=0
        ),
    )(hidden, filters, in_weight, out_weight, block_table)


def solution(mesh):
    return jax.shard_map(
        functools.partial(on_device, mesh.shape["seq"], mesh.shape["chan"]),
        mesh=mesh,
        in_specs=(P("seq", "chan"), P("seq", "chan"), P(None, None, "chan"), P("chan", None), P()),
        out_specs=P("seq", "chan"),
        check_vma=False,
    )
```

```python
import functools

import jax
import jax.numpy as jnp
from jax import lax
from jax.experimental import pallas as pl
from jax.experimental.pallas import tpu as pltpu
from jax.sharding import PartitionSpec as P

MESH = pl.DeviceIdType.MESH
LANES = 128


def flip(value, bits):
    result, bit = value, 1
    while bit <= bits:
        if bits & bit:
            result = result + bit - 2 * bit * ((value // bit) % 2)
        bit *= 2
    return result


def kernel(
    n_seq,
    n_chan,
    hidden_ref,
    filters_ref,
    win_ref,
    wout_ref,
    table_hbm,
    out_ref,
    table_ref,
    hbuf,
    fbuf,
    win,
    wout,
    streams,
    fpad,
    msend,
    mrecv,
    mwork,
    acc,
    gated,
    psend,
    precv,
    ssend,
    srecv,
    own_sem,
    win_sem,
    wout_sem,
    hz_send,
    hz_recv,
    hp_send,
    hp_recv,
    f_send,
    f_recv,
    m_send,
    m_recv,
    p_send,
    p_recv,
    s_send,
    s_recv,
):
    rows, chans = hidden_ref.shape
    seg = rows // 2
    tiles = seg // 8
    groups = chans // LANES
    n_z = n_chan // 2
    seq = lax.axis_index("seq")
    chan = lax.axis_index("chan")
    z = chan // 2
    core = chan % 2
    partner = 2 * z + 1 - core

    def chan_of(dz):
        return 2 * flip(z, dz) + core

    def lanes_of(which):
        return pl.ds(pl.multiple_of(which * chans, chans), chans)

    def remote(src, dst, send_sem, recv_sem, **where):
        return pltpu.make_async_remote_copy(
            src_ref=src,
            dst_ref=dst,
            send_sem=send_sem,
            recv_sem=recv_sem,
            device_id=where,
            device_id_type=MESH,
        )

    own_hidden = pltpu.make_async_copy(hidden_ref, hbuf.at[z, :, lanes_of(core)], own_sem.at[0])
    own_filters = pltpu.make_async_copy(filters_ref, fbuf.at[seq], own_sem.at[1])
    own_table = pltpu.make_async_copy(table_hbm, table_ref, own_sem.at[2])
    own_table.start()
    own_hidden.start()
    own_filters.start()
    win_copies = []
    for dz in range(n_z):
        part = pl.ds(pl.multiple_of(flip(z, dz) * 2 * chans, 2 * chans), 2 * chans)
        copy = pltpu.make_async_copy(win_ref.at[:, part, :], win.at[:, part, :], win_sem.at[dz])
        copy.start()
        win_copies.append(copy)
    wout_copy = pltpu.make_async_copy(wout_ref, wout, wout_sem)
    wout_copy.start()

    barrier = pltpu.get_barrier_semaphore()
    for ds in range(1, n_seq):
        pl.semaphore_signal(barrier, inc=1, device_id={"seq": flip(seq, ds)}, device_id_type=MESH)
    for dz in range(1, n_z):
        pl.semaphore_signal(barrier, inc=1, device_id={"chan": chan_of(dz)}, device_id_type=MESH)
    pl.semaphore_signal(barrier, inc=1, device_id={"chan": partner}, device_id_type=MESH)
    pl.semaphore_wait(barrier, n_seq - 1 + n_z)

    pending = []
    to_chip = {}
    for dz in range(n_z - 1, 0, -1):
        copy = remote(
            hidden_ref, hbuf.at[z, :, lanes_of(core)], hz_send.at[dz - 1], hz_recv.at[dz - 1], chan=chan_of(dz)
        )
        copy.start()
        to_chip[dz] = copy
        pending.append(copy)
    to_partner = {}
    to_partner[0] = remote(
        hidden_ref, hbuf.at[z, :, lanes_of(core)], hp_send.at[0], hp_recv.at[0], chan=partner
    )
    to_partner[0].start()
    pending.append(to_partner[0])
    filter_copies = []
    for ds in range(1, n_seq):
        copy = remote(filters_ref, fbuf.at[seq], f_send.at[ds - 1], f_recv.at[ds - 1], seq=flip(seq, ds))
        copy.start()
        filter_copies.append(copy)
        pending.append(copy)

    def project(dz, which):
        chip = flip(z, dz)
        part = pl.ds(pl.multiple_of(chip * 2 * chans, 2 * chans), 2 * chans)
        total = jnp.dot(hbuf[chip], win[which, part, :], preferred_element_type=jnp.float32)
        if dz == 0:
            streams[which] = total
        else:
            streams[which] += total

    def unpack_filters():
        own_filters.wait()
        for copy in filter_copies:
            copy.wait_recv()
        for group in range(groups):
            lanes = slice(group * LANES, (group + 1) * LANES)
            fpad[group, 0:seg, :] = jnp.zeros((seg, LANES), jnp.float32)
            for piece in range(n_seq):
                fpad[group, seg + piece * rows : seg + (piece + 1) * rows, :] = fbuf[piece, :, lanes].astype(
                    jnp.float32
                )

    own_hidden.wait()
    for dz in range(n_z):
        if dz:
            chip = flip(z, dz)
            to_chip[dz].wait_recv()
            spot = hbuf.at[chip, :, lanes_of(core)]
            to_partner[dz] = remote(spot, spot, hp_send.at[dz], hp_recv.at[dz], chan=partner)
            to_partner[dz].start()
            pending.append(to_partner[dz])
        if dz == n_z - 1:
            unpack_filters()
        to_partner[dz].wait_recv()
        win_copies[dz].wait()
        project(dz, 1)
        project(dz, 2)
        if dz < n_z - 1:
            project(dz, 0)

    own_table.wait()
    first = table_ref[2 * seq]
    second = table_ref[2 * seq + 1]
    early = jnp.minimum(first, second)
    in_order = jnp.full((seg, LANES), first) < jnp.full((seg, LANES), second)
    for group in range(groups):
        lanes = slice(group * LANES, (group + 1) * LANES)
        product = streams[1, :, lanes] * streams[2, :, lanes]
        lead = jnp.where(in_order, product[:seg], product[seg:])
        tail = jnp.where(in_order, product[seg:], product[:seg])
        mwork[0, group] = lead
        mwork[1, group] = tail
        msend[0:seg, lanes] = lead.astype(jnp.bfloat16)
        msend[seg : 2 * seg, lanes] = tail.astype(jnp.bfloat16)
    m_copies = []
    for ds in range(1, n_seq):
        copy = remote(msend, mrecv.at[ds - 1], m_send.at[ds - 1], m_recv.at[ds - 1], seq=flip(seq, ds))
        copy.start()
        m_copies.append(copy)
        pending.append(copy)
    project(n_z - 1, 0)

    def convolve(totals, group, slot, lag, lower=False):
        base = lag * seg + seg
        totals = list(totals)
        for shift in range(8):
            window = {}
            for gap in range(0 if lower else 1 - tiles, tiles):
                window[gap] = fpad[group, pl.ds(base + (8 * gap - shift), 8), :]
            for b in range(tiles):
                row = 8 * b + shift
                value = jnp.broadcast_to(mwork[slot, group, row : row + 1, :], (8, LANES))
                for a in range(b if lower else 0, tiles):
                    totals[a] = totals[a] + window[a - b] * value
        return totals

    def zeros():
        return [jnp.zeros((8, LANES), jnp.float32) for _ in range(tiles)]

    count = 2 * n_seq

    def own_blocks(group, carry):
        lead = convolve(zeros(), group, 0, 0, lower=True)
        tail = convolve(zeros(), group, 1, 0, lower=True)
        tail = convolve(tail, group, 0, count - 1 - 2 * early)
        for a in range(tiles):
            acc[0, group, 8 * a : 8 * a + 8, :] = lead[a]
            acc[1, group, 8 * a : 8 * a + 8, :] = tail[a]
        return carry

    lax.fori_loop(0, groups, own_blocks, 0)

    for ds in range(1, n_seq):
        other = flip(seq, ds)
        theirs = jnp.minimum(table_ref[2 * other], table_ref[2 * other + 1])
        m_copies[ds - 1].wait_recv()
        later = jnp.full((seg, LANES), early) > jnp.full((seg, LANES), theirs)
        later_tile = jnp.full((8, LANES), early) > jnp.full((8, LANES), theirs)
        for group in range(groups):
            lanes = slice(group * LANES, (group + 1) * LANES)
            lead = mrecv[ds - 1, 0:seg, lanes].astype(jnp.float32)
            tail = mrecv[ds - 1, seg : 2 * seg, lanes].astype(jnp.float32)
            mwork[0, group] = lead
            mwork[1, group] = jnp.where(later, lead, tail)

        def other_blocks(group, carry):
            tail = [acc[1, group, 8 * a : 8 * a + 8, :] for a in range(tiles)]
            tail = convolve(tail, group, 0, count - 1 - early - theirs)
            mixed = convolve(zeros(), group, 1, jnp.maximum(early, theirs) - jnp.minimum(early, theirs))
            for a in range(tiles):
                place = slice(8 * a, 8 * a + 8)
                acc[0, group, place, :] += jnp.where(later_tile, mixed[a], 0.0)
                acc[1, group, place, :] = tail[a] + jnp.where(later_tile, 0.0, mixed[a])
            return carry

        lax.fori_loop(0, groups, other_blocks, 0)

    for group in range(groups):
        lanes = slice(group * LANES, (group + 1) * LANES)
        lead = acc[0, group]
        tail = acc[1, group]
        gated[0:seg, lanes] = (streams[0, 0:seg, lanes] * jnp.where(in_order, lead, tail)).astype(jnp.bfloat16)
        gated[seg : 2 * seg, lanes] = (
            streams[0, seg : 2 * seg, lanes] * jnp.where(in_order, tail, lead)
        ).astype(jnp.bfloat16)

    wout_copy.wait()
    order = list(range(n_z - 1, -1, -1))
    p_copies = {}
    for dz in order:
        columns = lanes_of(2 * flip(z, dz) + 1 - core)
        psend[dz] = jnp.dot(gated[...], wout[:, columns], preferred_element_type=jnp.float32).astype(
            jnp.bfloat16
        )
        p_copies[dz] = remote(psend.at[dz], precv.at[dz], p_send.at[dz], p_recv.at[dz], chan=partner)
        p_copies[dz].start()
        pending.append(p_copies[dz])
    s_copies = []
    for dz in order:
        columns = lanes_of(chan_of(dz))
        share = jnp.dot(gated[...], wout[:, columns], preferred_element_type=jnp.float32)
        p_copies[dz].wait_recv()
        share = share + precv[dz].astype(jnp.float32)
        if dz:
            ssend[dz - 1] = share.astype(jnp.bfloat16)
            copy = remote(
                ssend.at[dz - 1], srecv.at[dz - 1], s_send.at[dz - 1], s_recv.at[dz - 1], chan=chan_of(dz)
            )
            copy.start()
            s_copies.append(copy)
            pending.append(copy)
        else:
            streams[0] = share
    for copy in s_copies:
        copy.wait_recv()
    total = streams[0]
    for dz in range(1, n_z):
        total = total + srecv[dz - 1].astype(jnp.float32)
    out_ref[...] = total.astype(jnp.bfloat16)
    for copy in pending:
        copy.wait_send()


def on_device(n_seq, n_chan, hidden, filters, in_weight, out_weight, block_table):
    rows, chans = hidden.shape
    seg = rows // 2
    groups = chans // LANES
    n_z = n_chan // 2
    width = in_weight.shape[1]
    bf16, f32 = jnp.bfloat16, jnp.float32
    dma = pltpu.SemaphoreType.DMA
    in_hbm = pl.BlockSpec(memory_space=pltpu.HBM)
    return pl.pallas_call(
        functools.partial(kernel, n_seq, n_chan),
        out_shape=jax.ShapeDtypeStruct((rows, chans), bf16),
        in_specs=[in_hbm] * 5,
        out_specs=pl.BlockSpec(memory_space=pltpu.VMEM),
        scratch_shapes=[
            pltpu.SMEM(block_table.shape, jnp.int32),
            pltpu.VMEM((n_z, rows, 2 * chans), bf16),
            pltpu.VMEM((n_seq, rows, chans), bf16),
            pltpu.VMEM((3, width, chans), bf16),
            pltpu.VMEM((chans, width), bf16),
            pltpu.VMEM((3, rows, chans), f32),
            pltpu.VMEM((groups, seg + n_seq * rows, LANES), f32),
            pltpu.VMEM((rows, chans), bf16),
            pltpu.VMEM((n_seq - 1, rows, chans), bf16),
            pltpu.VMEM((2, groups, seg, LANES), f32),
            pltpu.VMEM((2, groups, seg, LANES), f32),
            pltpu.VMEM((rows, chans), bf16),
            pltpu.VMEM((n_z, rows, chans), bf16),
            pltpu.VMEM((n_z, rows, chans), bf16),
            pltpu.VMEM((n_z - 1, rows, chans), bf16),
            pltpu.VMEM((n_z - 1, rows, chans), bf16),
            dma((3,)),
            dma((n_z,)),
            dma,
            dma((n_z - 1,)),
            dma((n_z - 1,)),
            dma((n_z,)),
            dma((n_z,)),
            dma((n_seq - 1,)),
            dma((n_seq - 1,)),
            dma((n_seq - 1,)),
            dma((n_seq - 1,)),
            dma((n_z,)),
            dma((n_z,)),
            dma((n_z - 1,)),
            dma((n_z - 1,)),
        ],
        compiler_params=pltpu.CompilerParams(
            collective_id=0, has_side_effects=True, vmem_limit_bytes=64 * 1024 * 1024
        ),
        cost_estimate=pl.CostEstimate(
            flops=8 * rows * width * chans, bytes_accessed=8 * width * chans, transcendentals=0
        ),
    )(hidden, filters, in_weight, out_weight, block_table)


def solution(mesh):
    return jax.shard_map(
        functools.partial(on_device, mesh.shape["seq"], mesh.shape["chan"]),
        mesh=mesh,
        in_specs=(P("seq", "chan"), P("seq", "chan"), P(None, None, "chan"), P("chan", None), P()),
        out_specs=P("seq", "chan"),
        check_vma=False,
    )
```

```python
import functools

import jax
import jax.numpy as jnp
from jax import lax
from jax.experimental import pallas as pl
from jax.experimental.pallas import tpu as pltpu
from jax.sharding import PartitionSpec as P

MESH = pl.DeviceIdType.MESH
LANES = 128


def flip(value, bits):
    result, bit = value, 1
    while bit <= bits:
        if bits & bit:
            result = result + bit - 2 * bit * ((value // bit) % 2)
        bit *= 2
    return result


def kernel(
    n_seq,
    n_chan,
    hidden_ref,
    filters_ref,
    win_ref,
    wout_ref,
    table_hbm,
    out_ref,
    table_ref,
    held,
    ordered,
    hbuf,
    fbuf,
    win,
    wout,
    streams,
    fpad,
    msend,
    mrecv,
    mwork,
    acc,
    gated,
    psend,
    precv,
    ssend,
    srecv,
    share_own,
    own_sem,
    win_sem,
    wout_sem,
    hz_send,
    hz_recv,
    hp_send,
    hp_recv,
    f_send,
    f_recv,
    m_send,
    m_recv,
    p_send,
    p_recv,
    s_send,
    s_recv,
):
    rows, chans = hidden_ref.shape
    seg = rows // 2
    tiles = seg // 8
    groups = chans // LANES
    n_z = n_chan // 2
    seq = lax.axis_index("seq")
    chan = lax.axis_index("chan")
    z = chan // 2
    core = chan % 2
    partner = 2 * z + 1 - core

    def chan_of(dz):
        return 2 * flip(z, dz) + core

    def lanes_of(which):
        return pl.ds(pl.multiple_of(which * chans, chans), chans)

    pending = []

    def send(src, dst, send_sem, recv_sem, **where):
        copy = pltpu.make_async_remote_copy(
            src_ref=src,
            dst_ref=dst,
            send_sem=send_sem,
            recv_sem=recv_sem,
            device_id=where,
            device_id_type=MESH,
        )
        copy.start()
        pending.append(copy)
        return copy

    own_table = pltpu.make_async_copy(table_hbm, table_ref, own_sem.at[0])
    own_hidden = pltpu.make_async_copy(hidden_ref, held, own_sem.at[1])
    own_filters = pltpu.make_async_copy(filters_ref, fbuf.at[seq], own_sem.at[2])
    own_table.start()
    own_hidden.start()

    barrier = pltpu.get_barrier_semaphore()
    for ds in range(1, n_seq):
        pl.semaphore_signal(barrier, inc=1, device_id={"seq": flip(seq, ds)}, device_id_type=MESH)
    for dz in range(1, n_z):
        pl.semaphore_signal(barrier, inc=1, device_id={"chan": chan_of(dz)}, device_id_type=MESH)
    pl.semaphore_signal(barrier, inc=1, device_id={"chan": partner}, device_id_type=MESH)

    win_copies = []
    for dz in range(n_z):
        part = pl.ds(pl.multiple_of(flip(z, dz) * 2 * chans, 2 * chans), 2 * chans)
        copy = pltpu.make_async_copy(win_ref.at[:, part, :], win.at[:, part, :], win_sem.at[dz])
        copy.start()
        win_copies.append(copy)
    own_filters.start()
    wout_copy = pltpu.make_async_copy(wout_ref, wout, wout_sem)
    wout_copy.start()

    own_table.wait()
    first = table_ref[2 * seq]
    second = table_ref[2 * seq + 1]
    early = jnp.minimum(first, second)

    def in_order(shape):
        return jnp.full(shape, first) < jnp.full(shape, second)

    own_hidden.wait()
    for group in range(groups):
        lanes = slice(group * LANES, (group + 1) * LANES)
        top = held[0:seg, lanes].astype(jnp.float32)
        bottom = held[seg:rows, lanes].astype(jnp.float32)
        keep = in_order((seg, LANES))
        ordered[0, :, lanes] = jnp.where(keep, top, bottom).astype(jnp.bfloat16)
        ordered[1, :, lanes] = jnp.where(keep, bottom, top).astype(jnp.bfloat16)
    for half in range(2):
        hbuf[half, z, :, lanes_of(core)] = ordered[half]
    pl.semaphore_wait(barrier, n_seq - 1 + n_z)

    to_chip, to_partner = {}, {}
    for half in range(2):
        for dz in range(n_z - 1, 0, -1):
            to_chip[half, dz] = send(
                ordered.at[half],
                hbuf.at[half, z, :, lanes_of(core)],
                hz_send.at[half, dz - 1],
                hz_recv.at[half, dz - 1],
                chan=chan_of(dz),
            )
        to_partner[half, 0] = send(
            ordered.at[half],
            hbuf.at[half, z, :, lanes_of(core)],
            hp_send.at[half, 0],
            hp_recv.at[half, 0],
            chan=partner,
        )
    filter_copies = [
        send(filters_ref, fbuf.at[seq], f_send.at[ds - 1], f_recv.at[ds - 1], seq=flip(seq, ds))
        for ds in range(1, n_seq)
    ]

    def project(half, dz, which):
        chip = flip(z, dz)
        part = pl.ds(pl.multiple_of(chip * 2 * chans, 2 * chans), 2 * chans)
        total = jnp.dot(hbuf[half, chip], win[which, part, :], preferred_element_type=jnp.float32)
        if dz == 0:
            streams[half, which] = total
        else:
            streams[half, which] += total

    m_copies = {}

    def keys_values(half):
        for dz in range(n_z):
            if dz:
                to_chip[half, dz].wait_recv()
                spot = hbuf.at[half, flip(z, dz), :, lanes_of(core)]
                to_partner[half, dz] = send(
                    spot, spot, hp_send.at[half, dz], hp_recv.at[half, dz], chan=partner
                )
            to_partner[half, dz].wait_recv()
            if half == 0:
                win_copies[dz].wait()
            project(half, dz, 1)
            project(half, dz, 2)
        for group in range(groups):
            lanes = slice(group * LANES, (group + 1) * LANES)
            product = streams[half, 1, :, lanes] * streams[half, 2, :, lanes]
            mwork[half, group] = product
            msend[half, :, lanes] = product.astype(jnp.bfloat16)
        for ds in range(1, n_seq):
            m_copies[half, ds] = send(
                msend.at[half],
                mrecv.at[half, ds - 1],
                m_send.at[half, ds - 1],
                m_recv.at[half, ds - 1],
                seq=flip(seq, ds),
            )

    def queries(half):
        for dz in range(n_z):
            project(half, dz, 0)

    def unpack_filters():
        own_filters.wait()
        for copy in filter_copies:
            copy.wait_recv()
        for group in range(groups):
            lanes = slice(group * LANES, (group + 1) * LANES)
            fpad[group, 0 : 2 * seg, :] = jnp.zeros((2 * seg, LANES), jnp.float32)
            for piece in range(n_seq):
                place = slice(2 * seg + piece * rows, 2 * seg + (piece + 1) * rows)
                fpad[group, place, :] = fbuf[piece, :, lanes].astype(jnp.float32)

    def convolve(targets, group, slot, lower=False):
        targets = [(jnp.maximum(lag, -1) * seg + 2 * seg, list(totals)) for lag, totals in targets]
        for shift in range(8):
            values = []
            for b in range(tiles):
                row = 8 * b + shift
                values.append(jnp.broadcast_to(mwork[slot, group, row : row + 1, :], (8, LANES)))
            for base, totals in targets:
                for gap in range(0 if lower else 1 - tiles, tiles):
                    window = fpad[group, pl.ds(base + (8 * gap - shift), 8), :]
                    for b in range(tiles):
                        if 0 <= b + gap < tiles:
                            totals[b + gap] = totals[b + gap] + window * values[b]
        return [totals for _, totals in targets]

    def zeros():
        return [jnp.zeros((8, LANES), jnp.float32) for _ in range(tiles)]

    def load_acc(half, group):
        return [acc[half, group, 8 * a : 8 * a + 8, :] for a in range(tiles)]

    def store_acc(half, group, totals):
        for a in range(tiles):
            acc[half, group, 8 * a : 8 * a + 8, :] = totals[a]

    count = 2 * n_seq
    zero = early * 0

    def own_early(group, carry):
        (lead,) = convolve([(zero, zeros())], group, 0, lower=True)
        (tail,) = convolve([(count - 1 - 2 * early, zeros())], group, 0)
        store_acc(0, group, lead)
        store_acc(1, group, tail)
        return carry

    def own_late(group, carry):
        (tail,) = convolve([(zero, load_acc(1, group))], group, 1, lower=True)
        store_acc(1, group, tail)
        return carry

    def receive(half, ds):
        m_copies[half, ds].wait_recv()
        for group in range(groups):
            lanes = slice(group * LANES, (group + 1) * LANES)
            mwork[1 + ds, group] = mrecv[half, ds - 1, :, lanes].astype(jnp.float32)
        other = flip(seq, ds)
        return jnp.minimum(table_ref[2 * other], table_ref[2 * other + 1])

    def other_early(ds):
        theirs = receive(0, ds)

        def body(group, carry):
            lead, tail = convolve(
                [(early - theirs, load_acc(0, group)), (count - 1 - early - theirs, load_acc(1, group))],
                group,
                1 + ds,
            )
            store_acc(0, group, lead)
            store_acc(1, group, tail)
            return carry

        lax.fori_loop(0, groups, body, 0)

    def other_late(ds):
        theirs = receive(1, ds)

        def body(group, carry):
            (tail,) = convolve([(theirs - early, load_acc(1, group))], group, 1 + ds)
            store_acc(1, group, tail)
            return carry

        lax.fori_loop(0, groups, body, 0)

    order = list(range(n_z - 1, -1, -1))
    p_copies, s_copies = {}, {}

    def for_partner(half):
        for group in range(groups):
            lanes = slice(group * LANES, (group + 1) * LANES)
            gated[half, :, lanes] = (streams[half, 0, :, lanes] * acc[half, group]).astype(jnp.bfloat16)
        for dz in order:
            columns = lanes_of(2 * flip(z, dz) + 1 - core)
            share = jnp.dot(gated[half], wout[:, columns], preferred_element_type=jnp.float32)
            psend[half, dz] = share.astype(jnp.bfloat16)
            p_copies[half, dz] = send(
                psend.at[half, dz],
                precv.at[half, dz],
                p_send.at[half, dz],
                p_recv.at[half, dz],
                chan=partner,
            )

    def for_chips(half):
        for dz in order:
            share = jnp.dot(gated[half], wout[:, lanes_of(chan_of(dz))], preferred_element_type=jnp.float32)
            p_copies[half, dz].wait_recv()
            share = share + precv[half, dz].astype(jnp.float32)
            if dz:
                ssend[half, dz - 1] = share.astype(jnp.bfloat16)
                s_copies[half, dz] = send(
                    ssend.at[half, dz - 1],
                    srecv.at[half, dz - 1],
                    s_send.at[half, dz - 1],
                    s_recv.at[half, dz - 1],
                    chan=chan_of(dz),
                )
            else:
                share_own[half] = share

    def add_up(half):
        total = share_own[half]
        for dz in range(1, n_z):
            s_copies[half, dz].wait_recv()
            total = total + srecv[half, dz - 1].astype(jnp.float32)
        return total

    keys_values(0)
    queries(0)
    unpack_filters()
    lax.fori_loop(0, groups, own_early, 0)
    keys_values(1)
    for ds in range(1, n_seq):
        other_early(ds)
    wout_copy.wait()
    for_partner(0)
    queries(1)
    lax.fori_loop(0, groups, own_late, 0)
    for_chips(0)
    for ds in range(1, n_seq):
        other_late(ds)
    for_partner(1)
    for_chips(1)
    lead = add_up(0)
    tail = add_up(1)
    keep = in_order((seg, chans))
    out_ref[0:seg, :] = jnp.where(keep, lead, tail).astype(jnp.bfloat16)
    out_ref[seg:rows, :] = jnp.where(keep, tail, lead).astype(jnp.bfloat16)
    for copy in pending:
        copy.wait_send()


def on_device(n_seq, n_chan, hidden, filters, in_weight, out_weight, block_table):
    rows, chans = hidden.shape
    seg = rows // 2
    groups = chans // LANES
    n_z = n_chan // 2
    width = in_weight.shape[1]
    bf16, f32 = jnp.bfloat16, jnp.float32
    dma = pltpu.SemaphoreType.DMA
    in_hbm = pl.BlockSpec(memory_space=pltpu.HBM)
    return pl.pallas_call(
        functools.partial(kernel, n_seq, n_chan),
        out_shape=jax.ShapeDtypeStruct((rows, chans), bf16),
        in_specs=[in_hbm] * 5,
        out_specs=pl.BlockSpec(memory_space=pltpu.VMEM),
        scratch_shapes=[
            pltpu.SMEM(block_table.shape, jnp.int32),
            pltpu.VMEM((rows, chans), bf16),
            pltpu.VMEM((2, seg, chans), bf16),
            pltpu.VMEM((2, n_z, seg, 2 * chans), bf16),
            pltpu.VMEM((n_seq, rows, chans), bf16),
            pltpu.VMEM((3, width, chans), bf16),
            pltpu.VMEM((chans, width), bf16),
            pltpu.VMEM((2, 3, seg, chans), f32),
            pltpu.VMEM((groups, 2 * seg + n_seq * rows, LANES), f32),
            pltpu.VMEM((2, seg, chans), bf16),
            pltpu.VMEM((2, n_seq - 1, seg, chans), bf16),
            pltpu.VMEM((n_seq + 1, groups, seg, LANES), f32),
            pltpu.VMEM((2, groups, seg, LANES), f32),
            pltpu.VMEM((2, seg, chans), bf16),
            pltpu.VMEM((2, n_z, seg, chans), bf16),
            pltpu.VMEM((2, n_z, seg, chans), bf16),
            pltpu.VMEM((2, n_z - 1, seg, chans), bf16),
            pltpu.VMEM((2, n_z - 1, seg, chans), bf16),
            pltpu.VMEM((2, seg, chans), f32),
            dma((3,)),
            dma((n_z,)),
            dma,
            dma((2, n_z - 1)),
            dma((2, n_z - 1)),
            dma((2, n_z)),
            dma((2, n_z)),
            dma((n_seq - 1,)),
            dma((n_seq - 1,)),
            dma((2, n_seq - 1)),
            dma((2, n_seq - 1)),
            dma((2, n_z)),
            dma((2, n_z)),
            dma((2, n_z - 1)),
            dma((2, n_z - 1)),
        ],
        compiler_params=pltpu.CompilerParams(
            collective_id=0, has_side_effects=True, vmem_limit_bytes=64 * 1024 * 1024
        ),
        cost_estimate=pl.CostEstimate(
            flops=8 * rows * width * chans, bytes_accessed=8 * width * chans, transcendentals=0
        ),
    )(hidden, filters, in_weight, out_weight, block_table)


def solution(mesh):
    return jax.shard_map(
        functools.partial(on_device, mesh.shape["seq"], mesh.shape["chan"]),
        mesh=mesh,
        in_specs=(P("seq", "chan"), P("seq", "chan"), P(None, None, "chan"), P("chan", None), P()),
        out_specs=P("seq", "chan"),
        check_vma=False,
    )
```

```python
import functools

import jax
import jax.numpy as jnp
from jax import lax
from jax.experimental import pallas as pl
from jax.experimental.pallas import tpu as pltpu
from jax.sharding import PartitionSpec as P

MESH = pl.DeviceIdType.MESH
LANES = 128


def flip(value, bits):
    result, bit = value, 1
    while bit <= bits:
        if bits & bit:
            result = result + bit - 2 * bit * ((value // bit) % 2)
        bit *= 2
    return result


def kernel(
    n_seq,
    n_chan,
    hidden_ref,
    filters_ref,
    win_ref,
    wout_ref,
    table_hbm,
    out_ref,
    table_ref,
    held,
    ordered,
    hbuf,
    fbuf,
    win,
    wout,
    streams,
    fpad,
    msend,
    mrecv,
    mwork,
    acc,
    gated,
    psend,
    precv,
    ssend,
    srecv,
    share_own,
    own_sem,
    win_sem,
    wout_sem,
    hz_send,
    hz_recv,
    hp_send,
    hp_recv,
    f_send,
    f_recv,
    m_send,
    m_recv,
    p_send,
    p_recv,
    s_send,
    s_recv,
):
    rows, chans = hidden_ref.shape
    seg = rows // 2
    tiles = seg // 8
    groups = chans // LANES
    n_z = n_chan // 2
    seq = lax.axis_index("seq")
    chan = lax.axis_index("chan")
    z = chan // 2
    core = chan % 2
    partner = 2 * z + 1 - core

    def chan_of(dz):
        return 2 * flip(z, dz) + core

    def lanes_of(which):
        return pl.ds(pl.multiple_of(which * chans, chans), chans)

    pending = []

    def send(src, dst, send_sem, recv_sem, **where):
        copy = pltpu.make_async_remote_copy(
            src_ref=src,
            dst_ref=dst,
            send_sem=send_sem,
            recv_sem=recv_sem,
            device_id=where,
            device_id_type=MESH,
        )
        copy.start()
        pending.append(copy)
        return copy

    own_table = pltpu.make_async_copy(table_hbm, table_ref, own_sem.at[0])
    own_hidden = pltpu.make_async_copy(hidden_ref, held, own_sem.at[1])
    own_filters = pltpu.make_async_copy(filters_ref, fbuf.at[seq], own_sem.at[2])
    own_table.start()
    own_hidden.start()

    barrier = pltpu.get_barrier_semaphore()
    for ds in range(1, n_seq):
        pl.semaphore_signal(barrier, inc=1, device_id={"seq": flip(seq, ds)}, device_id_type=MESH)
    for dz in range(1, n_z):
        pl.semaphore_signal(barrier, inc=1, device_id={"chan": chan_of(dz)}, device_id_type=MESH)
    pl.semaphore_signal(barrier, inc=1, device_id={"chan": partner}, device_id_type=MESH)

    kv_copies, q_copies = [], []
    for dz in range(n_z):
        part = pl.ds(pl.multiple_of(flip(z, dz) * 2 * chans, 2 * chans), 2 * chans)
        kv_copies.append(
            pltpu.make_async_copy(win_ref.at[1:3, part, :], win.at[1:3, part, :], win_sem.at[0, dz])
        )
        q_copies.append(
            pltpu.make_async_copy(win_ref.at[0:1, part, :], win.at[0:1, part, :], win_sem.at[1, dz])
        )
    for copy in kv_copies:
        copy.start()
    own_filters.start()
    wout_copy = pltpu.make_async_copy(wout_ref, wout, wout_sem)

    own_table.wait()
    first = table_ref[2 * seq]
    second = table_ref[2 * seq + 1]
    early = jnp.minimum(first, second)

    def in_order(shape):
        return jnp.full(shape, first) < jnp.full(shape, second)

    own_hidden.wait()
    for group in range(groups):
        lanes = slice(group * LANES, (group + 1) * LANES)
        top = held[0:seg, lanes].astype(jnp.float32)
        bottom = held[seg:rows, lanes].astype(jnp.float32)
        keep = in_order((seg, LANES))
        ordered[0:seg, lanes] = jnp.where(keep, top, bottom).astype(jnp.bfloat16)
        ordered[seg:rows, lanes] = jnp.where(keep, bottom, top).astype(jnp.bfloat16)
    hbuf[z, :, lanes_of(core)] = ordered[...]
    pl.semaphore_wait(barrier, n_seq - 1 + n_z)

    to_chip, to_partner = {}, {}
    for dz in range(n_z - 1, 0, -1):
        to_chip[dz] = send(
            ordered, hbuf.at[z, :, lanes_of(core)], hz_send.at[dz - 1], hz_recv.at[dz - 1], chan=chan_of(dz)
        )
    to_partner[0] = send(ordered, hbuf.at[z, :, lanes_of(core)], hp_send.at[0], hp_recv.at[0], chan=partner)
    filter_copies = [
        send(filters_ref, fbuf.at[seq], f_send.at[ds - 1], f_recv.at[ds - 1], seq=flip(seq, ds))
        for ds in range(1, n_seq)
    ]

    def project(dz, which):
        chip = flip(z, dz)
        part = pl.ds(pl.multiple_of(chip * 2 * chans, 2 * chans), 2 * chans)
        total = jnp.dot(hbuf[chip], win[which, part, :], preferred_element_type=jnp.float32)
        if dz == 0:
            streams[which] = total
        else:
            streams[which] += total

    m_copies = {}

    def keys_values():
        for dz in range(n_z):
            if dz:
                to_chip[dz].wait_recv()
                spot = hbuf.at[flip(z, dz), :, lanes_of(core)]
                to_partner[dz] = send(spot, spot, hp_send.at[dz], hp_recv.at[dz], chan=partner)
            to_partner[dz].wait_recv()
            kv_copies[dz].wait()
            project(dz, 1)
            project(dz, 2)
            if dz == 0:
                for copy in q_copies:
                    copy.start()
            if dz == min(1, n_z - 1):
                wout_copy.start()
        for half in range(2):
            part = slice(half * seg, (half + 1) * seg)
            for group in range(groups):
                lanes = slice(group * LANES, (group + 1) * LANES)
                product = streams[1, part, lanes] * streams[2, part, lanes]
                mwork[half, group] = product
                msend[half, :, lanes] = product.astype(jnp.bfloat16)
            for ds in range(1, n_seq):
                m_copies[half, ds] = send(
                    msend.at[half],
                    mrecv.at[half, ds - 1],
                    m_send.at[half, ds - 1],
                    m_recv.at[half, ds - 1],
                    seq=flip(seq, ds),
                )

    def queries():
        for dz in range(n_z):
            q_copies[dz].wait()
            project(dz, 0)

    def unpack_filters():
        own_filters.wait()
        for copy in filter_copies:
            copy.wait_recv()
        for group in range(groups):
            lanes = slice(group * LANES, (group + 1) * LANES)
            fpad[group, 0 : 2 * seg, :] = jnp.zeros((2 * seg, LANES), jnp.float32)
            for piece in range(n_seq):
                place = slice(2 * seg + piece * rows, 2 * seg + (piece + 1) * rows)
                fpad[group, place, :] = fbuf[piece, :, lanes].astype(jnp.float32)

    def convolve(targets, group, slot, lower=False):
        targets = [(jnp.maximum(lag, -1) * seg + 2 * seg, list(totals)) for lag, totals in targets]
        for shift in range(8):
            values = []
            for b in range(tiles):
                row = 8 * b + shift
                values.append(jnp.broadcast_to(mwork[slot, group, row : row + 1, :], (8, LANES)))
            for base, totals in targets:
                for gap in range(0 if lower else 1 - tiles, tiles):
                    window = fpad[group, pl.ds(base + (8 * gap - shift), 8), :]
                    for b in range(tiles):
                        if 0 <= b + gap < tiles:
                            totals[b + gap] = totals[b + gap] + window * values[b]
        return [totals for _, totals in targets]

    def zeros():
        return [jnp.zeros((8, LANES), jnp.float32) for _ in range(tiles)]

    def load_acc(half, group):
        return [acc[half, group, 8 * a : 8 * a + 8, :] for a in range(tiles)]

    def store_acc(half, group, totals):
        for a in range(tiles):
            acc[half, group, 8 * a : 8 * a + 8, :] = totals[a]

    count = 2 * n_seq
    zero = early * 0

    def own_early(group, carry):
        (lead,) = convolve([(zero, zeros())], group, 0, lower=True)
        (tail,) = convolve([(count - 1 - 2 * early, zeros())], group, 0)
        store_acc(0, group, lead)
        store_acc(1, group, tail)
        return carry

    def own_late(group, carry):
        (tail,) = convolve([(zero, load_acc(1, group))], group, 1, lower=True)
        store_acc(1, group, tail)
        return carry

    def receive(half, ds):
        m_copies[half, ds].wait_recv()
        for group in range(groups):
            lanes = slice(group * LANES, (group + 1) * LANES)
            mwork[1 + ds, group] = mrecv[half, ds - 1, :, lanes].astype(jnp.float32)
        other = flip(seq, ds)
        return jnp.minimum(table_ref[2 * other], table_ref[2 * other + 1])

    def other_early(ds):
        theirs = receive(0, ds)

        def body(group, carry):
            lead, tail = convolve(
                [(early - theirs, load_acc(0, group)), (count - 1 - early - theirs, load_acc(1, group))],
                group,
                1 + ds,
            )
            store_acc(0, group, lead)
            store_acc(1, group, tail)
            return carry

        lax.fori_loop(0, groups, body, 0)

    def other_late(ds):
        theirs = receive(1, ds)

        def body(group, carry):
            (tail,) = convolve([(theirs - early, load_acc(1, group))], group, 1 + ds)
            store_acc(1, group, tail)
            return carry

        lax.fori_loop(0, groups, body, 0)

    order = list(range(n_z - 1, -1, -1))
    p_copies, s_copies = {}, {}

    def for_partner():
        for half in range(2):
            part = slice(half * seg, (half + 1) * seg)
            for group in range(groups):
                lanes = slice(group * LANES, (group + 1) * LANES)
                gated[part, lanes] = (streams[0, part, lanes] * acc[half, group]).astype(jnp.bfloat16)
        for dz in order:
            columns = lanes_of(2 * flip(z, dz) + 1 - core)
            share = jnp.dot(gated[...], wout[:, columns], preferred_element_type=jnp.float32)
            psend[dz] = share.astype(jnp.bfloat16)
            p_copies[dz] = send(psend.at[dz], precv.at[dz], p_send.at[dz], p_recv.at[dz], chan=partner)

    def for_chips():
        for dz in order:
            share = jnp.dot(gated[...], wout[:, lanes_of(chan_of(dz))], preferred_element_type=jnp.float32)
            p_copies[dz].wait_recv()
            share = share + precv[dz].astype(jnp.float32)
            if dz:
                ssend[dz - 1] = share.astype(jnp.bfloat16)
                s_copies[dz] = send(
                    ssend.at[dz - 1], srecv.at[dz - 1], s_send.at[dz - 1], s_recv.at[dz - 1], chan=chan_of(dz)
                )
            else:
                share_own[...] = share

    keys_values()
    unpack_filters()
    lax.fori_loop(0, groups, own_early, 0)
    lax.fori_loop(0, groups, own_late, 0)
    queries()
    for ds in range(1, n_seq):
        other_early(ds)
    for ds in range(1, n_seq):
        other_late(ds)
    wout_copy.wait()
    for_partner()
    for_chips()
    total = share_own[...]
    for dz in range(1, n_z):
        s_copies[dz].wait_recv()
        total = total + srecv[dz - 1].astype(jnp.float32)
    lead = total[:seg]
    tail = total[seg:]
    keep = in_order((seg, chans))
    out_ref[0:seg, :] = jnp.where(keep, lead, tail).astype(jnp.bfloat16)
    out_ref[seg:rows, :] = jnp.where(keep, tail, lead).astype(jnp.bfloat16)
    for copy in pending:
        copy.wait_send()


def on_device(n_seq, n_chan, hidden, filters, in_weight, out_weight, block_table):
    rows, chans = hidden.shape
    seg = rows // 2
    groups = chans // LANES
    n_z = n_chan // 2
    width = in_weight.shape[1]
    bf16, f32 = jnp.bfloat16, jnp.float32
    dma = pltpu.SemaphoreType.DMA
    in_hbm = pl.BlockSpec(memory_space=pltpu.HBM)
    return pl.pallas_call(
        functools.partial(kernel, n_seq, n_chan),
        out_shape=jax.ShapeDtypeStruct((rows, chans), bf16),
        in_specs=[in_hbm] * 5,
        out_specs=pl.BlockSpec(memory_space=pltpu.VMEM),
        scratch_shapes=[
            pltpu.SMEM(block_table.shape, jnp.int32),
            pltpu.VMEM((rows, chans), bf16),
            pltpu.VMEM((rows, chans), bf16),
            pltpu.VMEM((n_z, rows, 2 * chans), bf16),
            pltpu.VMEM((n_seq, rows, chans), bf16),
            pltpu.VMEM((3, width, chans), bf16),
            pltpu.VMEM((chans, width), bf16),
            pltpu.VMEM((3, rows, chans), f32),
            pltpu.VMEM((groups, 2 * seg + n_seq * rows, LANES), f32),
            pltpu.VMEM((2, seg, chans), bf16),
            pltpu.VMEM((2, n_seq - 1, seg, chans), bf16),
            pltpu.VMEM((n_seq + 1, groups, seg, LANES), f32),
            pltpu.VMEM((2, groups, seg, LANES), f32),
            pltpu.VMEM((rows, chans), bf16),
            pltpu.VMEM((n_z, rows, chans), bf16),
            pltpu.VMEM((n_z, rows, chans), bf16),
            pltpu.VMEM((n_z - 1, rows, chans), bf16),
            pltpu.VMEM((n_z - 1, rows, chans), bf16),
            pltpu.VMEM((rows, chans), f32),
            dma((3,)),
            dma((2, n_z)),
            dma,
            dma((n_z - 1,)),
            dma((n_z - 1,)),
            dma((n_z,)),
            dma((n_z,)),
            dma((n_seq - 1,)),
            dma((n_seq - 1,)),
            dma((2, n_seq - 1)),
            dma((2, n_seq - 1)),
            dma((n_z,)),
            dma((n_z,)),
            dma((n_z - 1,)),
            dma((n_z - 1,)),
        ],
        compiler_params=pltpu.CompilerParams(
            collective_id=0, has_side_effects=True, vmem_limit_bytes=64 * 1024 * 1024
        ),
        cost_estimate=pl.CostEstimate(
            flops=8 * rows * width * chans, bytes_accessed=8 * width * chans, transcendentals=0
        ),
    )(hidden, filters, in_weight, out_weight, block_table)


def solution(mesh):
    return jax.shard_map(
        functools.partial(on_device, mesh.shape["seq"], mesh.shape["chan"]),
        mesh=mesh,
        in_specs=(P("seq", "chan"), P("seq", "chan"), P(None, None, "chan"), P("chan", None), P()),
        out_specs=P("seq", "chan"),
        check_vma=False,
    )
```

```python
import functools

import jax
import jax.numpy as jnp
from jax import lax
from jax.experimental import pallas as pl
from jax.experimental.pallas import tpu as pltpu
from jax.sharding import PartitionSpec as P

MESH = pl.DeviceIdType.MESH
LANES = 128


def flip(value, bits):
    result, bit = value, 1
    while bit <= bits:
        if bits & bit:
            result = result + bit - 2 * bit * ((value // bit) % 2)
        bit *= 2
    return result


def kernel(
    n_seq,
    n_chan,
    hidden_ref,
    filters_ref,
    win_ref,
    wout_ref,
    table_hbm,
    out_ref,
    table_ref,
    hbuf,
    fbuf,
    win,
    wout,
    streams,
    fpad,
    msend,
    mrecv,
    mwork,
    acc,
    gated,
    psend,
    precv,
    ssend,
    srecv,
    share_own,
    own_sem,
    win_sem,
    wout_sem,
    hz_send,
    hz_recv,
    hp_send,
    hp_recv,
    f_send,
    f_recv,
    m_send,
    m_recv,
    p_send,
    p_recv,
    s_send,
    s_recv,
):
    rows, chans = hidden_ref.shape
    seg = rows // 2
    tiles = seg // 8
    groups = chans // LANES
    n_z = n_chan // 2
    seq = lax.axis_index("seq")
    chan = lax.axis_index("chan")
    z = chan // 2
    core = chan % 2
    partner = 2 * z + 1 - core

    def chan_of(dz):
        return 2 * flip(z, dz) + core

    def lanes_of(which):
        return pl.ds(pl.multiple_of(which * chans, chans), chans)

    pending = []

    def send(src, dst, send_sem, recv_sem, **where):
        copy = pltpu.make_async_remote_copy(
            src_ref=src,
            dst_ref=dst,
            send_sem=send_sem,
            recv_sem=recv_sem,
            device_id=where,
            device_id_type=MESH,
        )
        copy.start()
        pending.append(copy)
        return copy

    own_table = pltpu.make_async_copy(table_hbm, table_ref, own_sem.at[0])
    own_hidden = pltpu.make_async_copy(hidden_ref, hbuf.at[z, :, lanes_of(core)], own_sem.at[1])
    own_filters = pltpu.make_async_copy(filters_ref, fbuf.at[seq], own_sem.at[2])
    own_table.start()
    own_hidden.start()

    barrier = pltpu.get_barrier_semaphore()
    for ds in range(1, n_seq):
        pl.semaphore_signal(barrier, inc=1, device_id={"seq": flip(seq, ds)}, device_id_type=MESH)
    for dz in range(1, n_z):
        pl.semaphore_signal(barrier, inc=1, device_id={"chan": chan_of(dz)}, device_id_type=MESH)
    pl.semaphore_signal(barrier, inc=1, device_id={"chan": partner}, device_id_type=MESH)

    kv_copies, q_copies = [], []
    for dz in range(n_z):
        part = pl.ds(pl.multiple_of(flip(z, dz) * 2 * chans, 2 * chans), 2 * chans)
        kv_copies.append(
            pltpu.make_async_copy(win_ref.at[1:3, part, :], win.at[1:3, part, :], win_sem.at[0, dz])
        )
        q_copies.append(
            pltpu.make_async_copy(win_ref.at[0:1, part, :], win.at[0:1, part, :], win_sem.at[1, dz])
        )
    for copy in kv_copies:
        copy.start()
    own_filters.start()
    wout_copy = pltpu.make_async_copy(wout_ref, wout, wout_sem)

    pl.semaphore_wait(barrier, n_seq - 1 + n_z)

    to_chip, to_partner = {}, {}
    for dz in range(n_z - 1, 0, -1):
        to_chip[dz] = send(
            hidden_ref, hbuf.at[z, :, lanes_of(core)], hz_send.at[dz - 1], hz_recv.at[dz - 1], chan=chan_of(dz)
        )
    to_partner[0] = send(hidden_ref, hbuf.at[z, :, lanes_of(core)], hp_send.at[0], hp_recv.at[0], chan=partner)
    filter_copies = [
        send(filters_ref, fbuf.at[seq], f_send.at[ds - 1], f_recv.at[ds - 1], seq=flip(seq, ds))
        for ds in range(1, n_seq)
    ]

    def project(dz, which):
        chip = flip(z, dz)
        part = pl.ds(pl.multiple_of(chip * 2 * chans, 2 * chans), 2 * chans)
        total = jnp.dot(hbuf[chip], win[which, part, :], preferred_element_type=jnp.float32)
        if dz == 0:
            streams[which] = total
        else:
            streams[which] += total

    m_copies = {}

    def keys_values():
        own_hidden.wait()
        for dz in range(n_z):
            if dz:
                to_chip[dz].wait_recv()
                spot = hbuf.at[flip(z, dz), :, lanes_of(core)]
                to_partner[dz] = send(spot, spot, hp_send.at[dz], hp_recv.at[dz], chan=partner)
            to_partner[dz].wait_recv()
            kv_copies[dz].wait()
            project(dz, 1)
            project(dz, 2)
            if dz == 0:
                for copy in q_copies:
                    copy.start()
            if dz == min(1, n_z - 1):
                wout_copy.start()

    def exchange():
        for half in range(2):
            for group in range(groups):
                lanes = slice(group * LANES, (group + 1) * LANES)
                product = streams[1, :, lanes] * streams[2, :, lanes]
                keep = in_order((seg, LANES))
                if half == 0:
                    product = jnp.where(keep, product[:seg], product[seg:])
                else:
                    product = jnp.where(keep, product[seg:], product[:seg])
                mwork[half, group] = product
                msend[half, :, lanes] = product.astype(jnp.bfloat16)
            for ds in range(1, n_seq):
                m_copies[half, ds] = send(
                    msend.at[half],
                    mrecv.at[half, ds - 1],
                    m_send.at[half, ds - 1],
                    m_recv.at[half, ds - 1],
                    seq=flip(seq, ds),
                )

    def queries():
        for dz in range(n_z):
            q_copies[dz].wait()
            project(dz, 0)

    def unpack_filters():
        own_filters.wait()
        for copy in filter_copies:
            copy.wait_recv()
        for group in range(groups):
            lanes = slice(group * LANES, (group + 1) * LANES)
            fpad[group, 0 : 2 * seg, :] = jnp.zeros((2 * seg, LANES), jnp.float32)
            for piece in range(n_seq):
                place = slice(2 * seg + piece * rows, 2 * seg + (piece + 1) * rows)
                fpad[group, place, :] = fbuf[piece, :, lanes].astype(jnp.float32)

    def convolve(targets, group, slot, lower=False):
        targets = [(jnp.maximum(lag, -1) * seg + 2 * seg, list(totals)) for lag, totals in targets]
        for shift in range(8):
            values = []
            for b in range(tiles):
                row = 8 * b + shift
                values.append(jnp.broadcast_to(mwork[slot, group, row : row + 1, :], (8, LANES)))
            for base, totals in targets:
                for gap in range(0 if lower else 1 - tiles, tiles):
                    window = fpad[group, pl.ds(base + (8 * gap - shift), 8), :]
                    for b in range(tiles):
                        if 0 <= b + gap < tiles:
                            totals[b + gap] = totals[b + gap] + window * values[b]
        return [totals for _, totals in targets]

    def zeros():
        return [jnp.zeros((8, LANES), jnp.float32) for _ in range(tiles)]

    def load_acc(half, group):
        return [acc[half, group, 8 * a : 8 * a + 8, :] for a in range(tiles)]

    def store_acc(half, group, totals):
        for a in range(tiles):
            acc[half, group, 8 * a : 8 * a + 8, :] = totals[a]

    count = 2 * n_seq

    def own_early(group, carry):
        (lead,) = convolve([(zero, zeros())], group, 0, lower=True)
        (tail,) = convolve([(count - 1 - 2 * early, zeros())], group, 0)
        store_acc(0, group, lead)
        store_acc(1, group, tail)
        return carry

    def own_late(group, carry):
        (tail,) = convolve([(zero, load_acc(1, group))], group, 1, lower=True)
        store_acc(1, group, tail)
        return carry

    def receive(half, ds):
        m_copies[half, ds].wait_recv()
        for group in range(groups):
            lanes = slice(group * LANES, (group + 1) * LANES)
            mwork[1 + ds, group] = mrecv[half, ds - 1, :, lanes].astype(jnp.float32)
        other = flip(seq, ds)
        return jnp.minimum(table_ref[2 * other], table_ref[2 * other + 1])

    def other_early(ds):
        theirs = receive(0, ds)

        def body(group, carry):
            lead, tail = convolve(
                [(early - theirs, load_acc(0, group)), (count - 1 - early - theirs, load_acc(1, group))],
                group,
                1 + ds,
            )
            store_acc(0, group, lead)
            store_acc(1, group, tail)
            return carry

        lax.fori_loop(0, groups, body, 0)

    def other_late(ds):
        theirs = receive(1, ds)

        def body(group, carry):
            (tail,) = convolve([(theirs - early, load_acc(1, group))], group, 1 + ds)
            store_acc(1, group, tail)
            return carry

        lax.fori_loop(0, groups, body, 0)

    order = list(range(n_z - 1, -1, -1))
    p_copies, s_copies = {}, {}

    def for_partner():
        for group in range(groups):
            lanes = slice(group * LANES, (group + 1) * LANES)
            keep = in_order((seg, LANES))
            lead = acc[0, group]
            tail = acc[1, group]
            top = streams[0, 0:seg, lanes] * jnp.where(keep, lead, tail)
            bottom = streams[0, seg:rows, lanes] * jnp.where(keep, tail, lead)
            gated[0:seg, lanes] = top.astype(jnp.bfloat16)
            gated[seg:rows, lanes] = bottom.astype(jnp.bfloat16)
        for dz in order:
            columns = lanes_of(2 * flip(z, dz) + 1 - core)
            share = jnp.dot(gated[...], wout[:, columns], preferred_element_type=jnp.float32)
            psend[dz] = share.astype(jnp.bfloat16)
            p_copies[dz] = send(psend.at[dz], precv.at[dz], p_send.at[dz], p_recv.at[dz], chan=partner)

    def for_chips():
        for dz in order:
            share = jnp.dot(gated[...], wout[:, lanes_of(chan_of(dz))], preferred_element_type=jnp.float32)
            p_copies[dz].wait_recv()
            share = share + precv[dz].astype(jnp.float32)
            if dz:
                ssend[dz - 1] = share.astype(jnp.bfloat16)
                s_copies[dz] = send(
                    ssend.at[dz - 1], srecv.at[dz - 1], s_send.at[dz - 1], s_recv.at[dz - 1], chan=chan_of(dz)
                )
            else:
                share_own[...] = share

    keys_values()
    own_table.wait()
    first = table_ref[2 * seq]
    second = table_ref[2 * seq + 1]
    early = jnp.minimum(first, second)
    zero = early * 0

    def in_order(shape):
        return jnp.full(shape, first) < jnp.full(shape, second)

    exchange()
    unpack_filters()
    lax.fori_loop(0, groups, own_early, 0)
    lax.fori_loop(0, groups, own_late, 0)
    queries()
    for ds in range(1, n_seq):
        other_early(ds)
    for ds in range(1, n_seq):
        other_late(ds)
    wout_copy.wait()
    for_partner()
    for_chips()
    total = share_own[...]
    for dz in range(1, n_z):
        s_copies[dz].wait_recv()
        total = total + srecv[dz - 1].astype(jnp.float32)
    out_ref[...] = total.astype(jnp.bfloat16)
    for copy in pending:
        copy.wait_send()


def on_device(n_seq, n_chan, hidden, filters, in_weight, out_weight, block_table):
    rows, chans = hidden.shape
    seg = rows // 2
    groups = chans // LANES
    n_z = n_chan // 2
    width = in_weight.shape[1]
    bf16, f32 = jnp.bfloat16, jnp.float32
    dma = pltpu.SemaphoreType.DMA
    in_hbm = pl.BlockSpec(memory_space=pltpu.HBM)
    return pl.pallas_call(
        functools.partial(kernel, n_seq, n_chan),
        out_shape=jax.ShapeDtypeStruct((rows, chans), bf16),
        in_specs=[in_hbm] * 5,
        out_specs=pl.BlockSpec(memory_space=pltpu.VMEM),
        scratch_shapes=[
            pltpu.SMEM(block_table.shape, jnp.int32),
            pltpu.VMEM((n_z, rows, 2 * chans), bf16),
            pltpu.VMEM((n_seq, rows, chans), bf16),
            pltpu.VMEM((3, width, chans), bf16),
            pltpu.VMEM((chans, width), bf16),
            pltpu.VMEM((3, rows, chans), f32),
            pltpu.VMEM((groups, 2 * seg + n_seq * rows, LANES), f32),
            pltpu.VMEM((2, seg, chans), bf16),
            pltpu.VMEM((2, n_seq - 1, seg, chans), bf16),
            pltpu.VMEM((n_seq + 1, groups, seg, LANES), f32),
            pltpu.VMEM((2, groups, seg, LANES), f32),
            pltpu.VMEM((rows, chans), bf16),
            pltpu.VMEM((n_z, rows, chans), bf16),
            pltpu.VMEM((n_z, rows, chans), bf16),
            pltpu.VMEM((n_z - 1, rows, chans), bf16),
            pltpu.VMEM((n_z - 1, rows, chans), bf16),
            pltpu.VMEM((rows, chans), f32),
            dma((3,)),
            dma((2, n_z)),
            dma,
            dma((n_z - 1,)),
            dma((n_z - 1,)),
            dma((n_z,)),
            dma((n_z,)),
            dma((n_seq - 1,)),
            dma((n_seq - 1,)),
            dma((2, n_seq - 1)),
            dma((2, n_seq - 1)),
            dma((n_z,)),
            dma((n_z,)),
            dma((n_z - 1,)),
            dma((n_z - 1,)),
        ],
        compiler_params=pltpu.CompilerParams(
            collective_id=0, has_side_effects=True, vmem_limit_bytes=64 * 1024 * 1024
        ),
        cost_estimate=pl.CostEstimate(
            flops=8 * rows * width * chans, bytes_accessed=8 * width * chans, transcendentals=0
        ),
    )(hidden, filters, in_weight, out_weight, block_table)


def solution(mesh):
    return jax.shard_map(
        functools.partial(on_device, mesh.shape["seq"], mesh.shape["chan"]),
        mesh=mesh,
        in_specs=(P("seq", "chan"), P("seq", "chan"), P(None, None, "chan"), P("chan", None), P()),
        out_specs=P("seq", "chan"),
        check_vma=False,
    )
```

```python
import functools

import jax
import jax.numpy as jnp
from jax import lax
from jax.experimental import pallas as pl
from jax.experimental.pallas import tpu as pltpu
from jax.sharding import PartitionSpec as P

MESH = pl.DeviceIdType.MESH
LANES = 128


def flip(value, bits):
    result, bit = value, 1
    while bit <= bits:
        if bits & bit:
            result = result + bit - 2 * bit * ((value // bit) % 2)
        bit *= 2
    return result


def kernel(
    n_seq,
    n_chan,
    hidden_ref,
    filters_ref,
    win_ref,
    wout_ref,
    table_hbm,
    out_ref,
    table_ref,
    hbuf,
    fbuf,
    win,
    wout,
    streams,
    fpad,
    msend,
    mrecv,
    mwork,
    acc,
    gated,
    psend,
    precv,
    ssend,
    srecv,
    share_own,
    own_sem,
    win_sem,
    wout_sem,
    hz_send,
    hz_recv,
    hp_send,
    hp_recv,
    f_send,
    f_recv,
    m_send,
    m_recv,
    p_send,
    p_recv,
    s_send,
    s_recv,
):
    rows, chans = hidden_ref.shape
    seg = rows // 2
    tiles = seg // 8
    groups = chans // LANES
    n_z = n_chan // 2
    seq = lax.axis_index("seq")
    chan = lax.axis_index("chan")
    z = chan // 2
    core = chan % 2
    partner = 2 * z + 1 - core

    def chan_of(dz):
        return 2 * flip(z, dz) + core

    def lanes_of(which):
        return pl.ds(pl.multiple_of(which * chans, chans), chans)

    pending = []

    def send(src, dst, send_sem, recv_sem, **where):
        copy = pltpu.make_async_remote_copy(
            src_ref=src,
            dst_ref=dst,
            send_sem=send_sem,
            recv_sem=recv_sem,
            device_id=where,
            device_id_type=MESH,
        )
        copy.start()
        pending.append(copy)
        return copy

    own_table = pltpu.make_async_copy(table_hbm, table_ref, own_sem.at[0])
    own_hidden = pltpu.make_async_copy(hidden_ref, hbuf.at[z, :, lanes_of(core)], own_sem.at[1])
    own_filters = pltpu.make_async_copy(filters_ref, fbuf.at[seq], own_sem.at[2])
    own_table.start()
    own_hidden.start()

    barrier = pltpu.get_barrier_semaphore()
    for ds in range(1, n_seq):
        pl.semaphore_signal(barrier, inc=1, device_id={"seq": flip(seq, ds)}, device_id_type=MESH)
    for dz in range(1, n_z):
        pl.semaphore_signal(barrier, inc=1, device_id={"chan": chan_of(dz)}, device_id_type=MESH)
    pl.semaphore_signal(barrier, inc=1, device_id={"chan": partner}, device_id_type=MESH)

    kv_copies, q_copies = [], []
    for dz in range(n_z):
        part = pl.ds(pl.multiple_of(flip(z, dz) * 2 * chans, 2 * chans), 2 * chans)
        kv_copies.append(
            pltpu.make_async_copy(win_ref.at[1:3, part, :], win.at[1:3, part, :], win_sem.at[0, dz])
        )
        q_copies.append(
            pltpu.make_async_copy(win_ref.at[0:1, part, :], win.at[0:1, part, :], win_sem.at[1, dz])
        )
    for copy in kv_copies:
        copy.start()
    own_filters.start()
    wout_copy = pltpu.make_async_copy(wout_ref, wout, wout_sem)

    pl.semaphore_wait(barrier, n_seq - 1 + n_z)

    to_chip, to_partner = {}, {}
    for dz in range(1, n_z):
        to_chip[dz] = send(
            hidden_ref, hbuf.at[z, :, lanes_of(core)], hz_send.at[dz - 1], hz_recv.at[dz - 1], chan=chan_of(dz)
        )
    to_partner[0] = send(hidden_ref, hbuf.at[z, :, lanes_of(core)], hp_send.at[0], hp_recv.at[0], chan=partner)
    filter_copies = [
        send(filters_ref, fbuf.at[seq], f_send.at[ds - 1], f_recv.at[ds - 1], seq=flip(seq, ds))
        for ds in range(1, n_seq)
    ]

    def project(dz, which, columns, add=True):
        chip = flip(z, dz)
        start = chip * 2 * chans + columns.start
        part = pl.ds(pl.multiple_of(start, chans), columns.size)
        total = jnp.dot(hbuf[chip, :, columns], win[which, part, :], preferred_element_type=jnp.float32)
        if add:
            total = streams[which] + total
        streams[which] = total

    m_copies = {}

    def keys_values():
        own_hidden.wait()
        for dz in range(n_z):
            if dz:
                to_chip[dz].wait_recv()
                spot = hbuf.at[flip(z, dz), :, lanes_of(core)]
                to_partner[dz] = send(spot, spot, hp_send.at[dz], hp_recv.at[dz], chan=partner)
            kv_copies[dz].wait()
            project(dz, 1, lanes_of(core), dz > 0)
            project(dz, 2, lanes_of(core), dz > 0)
            to_partner[dz].wait_recv()
            project(dz, 1, lanes_of(1 - core))
            project(dz, 2, lanes_of(1 - core))
            if dz == 0:
                for copy in q_copies:
                    copy.start()
            if dz == min(1, n_z - 1):
                wout_copy.start()

    def exchange():
        for half in range(2):
            for group in range(groups):
                lanes = slice(group * LANES, (group + 1) * LANES)
                product = streams[1, :, lanes] * streams[2, :, lanes]
                keep = in_order((seg, LANES))
                if half == 0:
                    product = jnp.where(keep, product[:seg], product[seg:])
                else:
                    product = jnp.where(keep, product[seg:], product[:seg])
                mwork[half, group] = product
                msend[half, :, lanes] = product.astype(jnp.bfloat16)
            for ds in range(1, n_seq):
                m_copies[half, ds] = send(
                    msend.at[half],
                    mrecv.at[half, ds - 1],
                    m_send.at[half, ds - 1],
                    m_recv.at[half, ds - 1],
                    seq=flip(seq, ds),
                )

    def queries():
        for dz in range(n_z):
            q_copies[dz].wait()
            project(dz, 0, pl.ds(0, 2 * chans), dz > 0)

    def unpack_filters():
        own_filters.wait()
        for copy in filter_copies:
            copy.wait_recv()
        for group in range(groups):
            lanes = slice(group * LANES, (group + 1) * LANES)
            fpad[group, 0 : 2 * seg, :] = jnp.zeros((2 * seg, LANES), jnp.float32)
            for piece in range(n_seq):
                place = slice(2 * seg + piece * rows, 2 * seg + (piece + 1) * rows)
                fpad[group, place, :] = fbuf[piece, :, lanes].astype(jnp.float32)

    def convolve(targets, group, slot, lower=False):
        targets = [(jnp.maximum(lag, -1) * seg + 2 * seg, list(totals)) for lag, totals in targets]
        for shift in range(8):
            values = []
            for b in range(tiles):
                row = 8 * b + shift
                values.append(jnp.broadcast_to(mwork[slot, group, row : row + 1, :], (8, LANES)))
            for base, totals in targets:
                for gap in range(0 if lower else 1 - tiles, tiles):
                    window = fpad[group, pl.ds(base + (8 * gap - shift), 8), :]
                    for b in range(tiles):
                        if 0 <= b + gap < tiles:
                            totals[b + gap] = totals[b + gap] + window * values[b]
        return [totals for _, totals in targets]

    def zeros():
        return [jnp.zeros((8, LANES), jnp.float32) for _ in range(tiles)]

    def load_acc(half, group):
        return [acc[half, group, 8 * a : 8 * a + 8, :] for a in range(tiles)]

    def store_acc(half, group, totals):
        for a in range(tiles):
            acc[half, group, 8 * a : 8 * a + 8, :] = totals[a]

    count = 2 * n_seq

    def own_early(group, carry):
        (lead,) = convolve([(zero, zeros())], group, 0, lower=True)
        (tail,) = convolve([(count - 1 - 2 * early, zeros())], group, 0)
        store_acc(0, group, lead)
        store_acc(1, group, tail)
        return carry

    def own_late(group, carry):
        (tail,) = convolve([(zero, load_acc(1, group))], group, 1, lower=True)
        store_acc(1, group, tail)
        return carry

    def receive(half, ds):
        m_copies[half, ds].wait_recv()
        for group in range(groups):
            lanes = slice(group * LANES, (group + 1) * LANES)
            mwork[1 + ds, group] = mrecv[half, ds - 1, :, lanes].astype(jnp.float32)
        other = flip(seq, ds)
        return jnp.minimum(table_ref[2 * other], table_ref[2 * other + 1])

    def other_early(ds):
        theirs = receive(0, ds)

        def body(group, carry):
            lead, tail = convolve(
                [(early - theirs, load_acc(0, group)), (count - 1 - early - theirs, load_acc(1, group))],
                group,
                1 + ds,
            )
            store_acc(0, group, lead)
            store_acc(1, group, tail)
            return carry

        lax.fori_loop(0, groups, body, 0)

    def other_late(ds):
        theirs = receive(1, ds)

        def body(group, carry):
            (tail,) = convolve([(theirs - early, load_acc(1, group))], group, 1 + ds)
            store_acc(1, group, tail)
            return carry

        lax.fori_loop(0, groups, body, 0)

    order = list(range(n_z - 1, -1, -1))
    p_copies, s_copies = {}, {}

    def for_partner():
        for group in range(groups):
            lanes = slice(group * LANES, (group + 1) * LANES)
            keep = in_order((seg, LANES))
            lead = acc[0, group]
            tail = acc[1, group]
            top = streams[0, 0:seg, lanes] * jnp.where(keep, lead, tail)
            bottom = streams[0, seg:rows, lanes] * jnp.where(keep, tail, lead)
            gated[0:seg, lanes] = top.astype(jnp.bfloat16)
            gated[seg:rows, lanes] = bottom.astype(jnp.bfloat16)
        for dz in order:
            columns = lanes_of(2 * flip(z, dz) + 1 - core)
            share = jnp.dot(gated[...], wout[:, columns], preferred_element_type=jnp.float32)
            psend[dz] = share.astype(jnp.bfloat16)
            p_copies[dz] = send(psend.at[dz], precv.at[dz], p_send.at[dz], p_recv.at[dz], chan=partner)

    def for_chips():
        for dz in order:
            share = jnp.dot(gated[...], wout[:, lanes_of(chan_of(dz))], preferred_element_type=jnp.float32)
            p_copies[dz].wait_recv()
            share = share + precv[dz].astype(jnp.float32)
            if dz:
                ssend[dz - 1] = share.astype(jnp.bfloat16)
                s_copies[dz] = send(
                    ssend.at[dz - 1], srecv.at[dz - 1], s_send.at[dz - 1], s_recv.at[dz - 1], chan=chan_of(dz)
                )
            else:
                share_own[...] = share

    keys_values()
    own_table.wait()
    first = table_ref[2 * seq]
    second = table_ref[2 * seq + 1]
    early = jnp.minimum(first, second)
    zero = early * 0

    def in_order(shape):
        return jnp.full(shape, first) < jnp.full(shape, second)

    exchange()
    unpack_filters()
    lax.fori_loop(0, groups, own_early, 0)
    lax.fori_loop(0, groups, own_late, 0)
    queries()
    for ds in range(1, n_seq):
        other_early(ds)
    for ds in range(1, n_seq):
        other_late(ds)
    wout_copy.wait()
    for_partner()
    for_chips()
    total = share_own[...]
    for dz in range(1, n_z):
        s_copies[dz].wait_recv()
        total = total + srecv[dz - 1].astype(jnp.float32)
    out_ref[...] = total.astype(jnp.bfloat16)
    for copy in pending:
        copy.wait_send()


def on_device(n_seq, n_chan, hidden, filters, in_weight, out_weight, block_table):
    rows, chans = hidden.shape
    seg = rows // 2
    groups = chans // LANES
    n_z = n_chan // 2
    width = in_weight.shape[1]
    bf16, f32 = jnp.bfloat16, jnp.float32
    dma = pltpu.SemaphoreType.DMA
    in_hbm = pl.BlockSpec(memory_space=pltpu.HBM)
    return pl.pallas_call(
        functools.partial(kernel, n_seq, n_chan),
        out_shape=jax.ShapeDtypeStruct((rows, chans), bf16),
        in_specs=[in_hbm] * 5,
        out_specs=pl.BlockSpec(memory_space=pltpu.VMEM),
        scratch_shapes=[
            pltpu.SMEM(block_table.shape, jnp.int32),
            pltpu.VMEM((n_z, rows, 2 * chans), bf16),
            pltpu.VMEM((n_seq, rows, chans), bf16),
            pltpu.VMEM((3, width, chans), bf16),
            pltpu.VMEM((chans, width), bf16),
            pltpu.VMEM((3, rows, chans), f32),
            pltpu.VMEM((groups, 2 * seg + n_seq * rows, LANES), f32),
            pltpu.VMEM((2, seg, chans), bf16),
            pltpu.VMEM((2, n_seq - 1, seg, chans), bf16),
            pltpu.VMEM((n_seq + 1, groups, seg, LANES), f32),
            pltpu.VMEM((2, groups, seg, LANES), f32),
            pltpu.VMEM((rows, chans), bf16),
            pltpu.VMEM((n_z, rows, chans), bf16),
            pltpu.VMEM((n_z, rows, chans), bf16),
            pltpu.VMEM((n_z - 1, rows, chans), bf16),
            pltpu.VMEM((n_z - 1, rows, chans), bf16),
            pltpu.VMEM((rows, chans), f32),
            dma((3,)),
            dma((2, n_z)),
            dma,
            dma((n_z - 1,)),
            dma((n_z - 1,)),
            dma((n_z,)),
            dma((n_z,)),
            dma((n_seq - 1,)),
            dma((n_seq - 1,)),
            dma((2, n_seq - 1)),
            dma((2, n_seq - 1)),
            dma((n_z,)),
            dma((n_z,)),
            dma((n_z - 1,)),
            dma((n_z - 1,)),
        ],
        compiler_params=pltpu.CompilerParams(
            collective_id=0, has_side_effects=True, vmem_limit_bytes=64 * 1024 * 1024
        ),
        cost_estimate=pl.CostEstimate(
            flops=8 * rows * width * chans, bytes_accessed=8 * width * chans, transcendentals=0
        ),
    )(hidden, filters, in_weight, out_weight, block_table)


def solution(mesh):
    return jax.shard_map(
        functools.partial(on_device, mesh.shape["seq"], mesh.shape["chan"]),
        mesh=mesh,
        in_specs=(P("seq", "chan"), P("seq", "chan"), P(None, None, "chan"), P("chan", None), P()),
        out_specs=P("seq", "chan"),
        check_vma=False,
    )
```

```python
import functools

import jax
import jax.numpy as jnp
from jax import lax
from jax.experimental import pallas as pl
from jax.experimental.pallas import tpu as pltpu
from jax.sharding import PartitionSpec as P

MESH = pl.DeviceIdType.MESH
LANES = 128


def flip(value, bits):
    result, bit = value, 1
    while bit <= bits:
        if bits & bit:
            result = result + bit - 2 * bit * ((value // bit) % 2)
        bit *= 2
    return result


def kernel(
    n_seq,
    n_chan,
    hidden_ref,
    filters_ref,
    win_ref,
    wout_ref,
    table_hbm,
    out_ref,
    table_ref,
    hbuf,
    fbuf,
    win,
    wout,
    streams,
    fpad,
    msend,
    mrecv,
    mwork,
    acc,
    gated,
    psend,
    precv,
    ssend,
    srecv,
    share_own,
    own_sem,
    win_sem,
    wout_sem,
    hz_send,
    hz_recv,
    hp_send,
    hp_recv,
    f_send,
    f_recv,
    m_send,
    m_recv,
    p_send,
    p_recv,
    s_send,
    s_recv,
):
    rows, chans = hidden_ref.shape
    seg = rows // 2
    tiles = seg // 8
    groups = chans // LANES
    n_z = n_chan // 2
    seq = lax.axis_index("seq")
    chan = lax.axis_index("chan")
    z = chan // 2
    core = chan % 2
    partner = 2 * z + 1 - core

    def chan_of(dz):
        return 2 * flip(z, dz) + core

    def lanes_of(which):
        return pl.ds(pl.multiple_of(which * chans, chans), chans)

    pending = []

    def send(src, dst, send_sem, recv_sem, **where):
        copy = pltpu.make_async_remote_copy(
            src_ref=src,
            dst_ref=dst,
            send_sem=send_sem,
            recv_sem=recv_sem,
            device_id=where,
            device_id_type=MESH,
        )
        copy.start()
        pending.append(copy)
        return copy

    own_table = pltpu.make_async_copy(table_hbm, table_ref, own_sem.at[0])
    own_hidden = pltpu.make_async_copy(hidden_ref, hbuf.at[z, :, lanes_of(core)], own_sem.at[1])
    own_filters = pltpu.make_async_copy(filters_ref, fbuf.at[seq], own_sem.at[2])
    own_table.start()
    own_hidden.start()

    barrier = pltpu.get_barrier_semaphore()
    for ds in range(1, n_seq):
        pl.semaphore_signal(barrier, inc=1, device_id={"seq": flip(seq, ds)}, device_id_type=MESH)
    for dz in range(1, n_z):
        pl.semaphore_signal(barrier, inc=1, device_id={"chan": chan_of(dz)}, device_id_type=MESH)
    pl.semaphore_signal(barrier, inc=1, device_id={"chan": partner}, device_id_type=MESH)

    kv_copies, q_copies = [], []
    for dz in range(n_z):
        part = pl.ds(pl.multiple_of(flip(z, dz) * 2 * chans, 2 * chans), 2 * chans)
        kv_copies.append(
            pltpu.make_async_copy(win_ref.at[1:3, part, :], win.at[1:3, part, :], win_sem.at[0, dz])
        )
        q_copies.append(
            pltpu.make_async_copy(win_ref.at[0:1, part, :], win.at[0:1, part, :], win_sem.at[1, dz])
        )
    for copy in kv_copies:
        copy.start()
    own_filters.start()
    wout_copy = pltpu.make_async_copy(wout_ref, wout, wout_sem)

    pl.semaphore_wait(barrier, n_seq - 1 + n_z)

    to_chip, to_partner = {}, {}
    for dz in range(1, n_z):
        to_chip[dz] = send(
            hidden_ref, hbuf.at[z, :, lanes_of(core)], hz_send.at[dz - 1], hz_recv.at[dz - 1], chan=chan_of(dz)
        )
    to_partner[0] = send(hidden_ref, hbuf.at[z, :, lanes_of(core)], hp_send.at[0], hp_recv.at[0], chan=partner)
    filter_copies = [
        send(filters_ref, fbuf.at[seq], f_send.at[ds - 1], f_recv.at[ds - 1], seq=flip(seq, ds))
        for ds in range(1, n_seq)
    ]

    def project(dz, which, columns, add=True):
        chip = flip(z, dz)
        start = chip * 2 * chans + columns.start
        part = pl.ds(pl.multiple_of(start, chans), columns.size)
        total = jnp.dot(hbuf[chip, :, columns], win[which, part, :], preferred_element_type=jnp.float32)
        if add:
            total = streams[which] + total
        streams[which] = total

    m_copies = {}

    def keys_values():
        own_hidden.wait()
        for dz in range(n_z):
            if dz:
                to_chip[dz].wait_recv()
                spot = hbuf.at[flip(z, dz), :, lanes_of(core)]
                to_partner[dz] = send(spot, spot, hp_send.at[dz], hp_recv.at[dz], chan=partner)
            kv_copies[dz].wait()
            project(dz, 1, lanes_of(core), dz > 0)
            project(dz, 2, lanes_of(core), dz > 0)
            to_partner[dz].wait_recv()
            project(dz, 1, lanes_of(1 - core))
            project(dz, 2, lanes_of(1 - core))
            if dz == 0:
                for copy in q_copies:
                    copy.start()
            if dz == min(1, n_z - 1):
                wout_copy.start()

    def exchange():
        for half in range(2):
            for group in range(groups):
                lanes = slice(group * LANES, (group + 1) * LANES)
                product = streams[1, :, lanes] * streams[2, :, lanes]
                keep = in_order((seg, LANES))
                if half == 0:
                    product = jnp.where(keep, product[:seg], product[seg:])
                else:
                    product = jnp.where(keep, product[seg:], product[:seg])
                mwork[half, group] = product
                msend[half, :, lanes] = product.astype(jnp.bfloat16)
            for ds in range(1, n_seq):
                m_copies[half, ds] = send(
                    msend.at[half],
                    mrecv.at[half, ds - 1],
                    m_send.at[half, ds - 1],
                    m_recv.at[half, ds - 1],
                    seq=flip(seq, ds),
                )

    def queries():
        for dz in range(n_z):
            q_copies[dz].wait()
            project(dz, 0, pl.ds(0, 2 * chans), dz > 0)

    def unpack_filters():
        own_filters.wait()
        for copy in filter_copies:
            copy.wait_recv()
        for group in range(groups):
            lanes = slice(group * LANES, (group + 1) * LANES)
            fpad[group, 0 : 2 * seg, :] = jnp.zeros((2 * seg, LANES), jnp.float32)
            for piece in range(n_seq):
                place = slice(2 * seg + piece * rows, 2 * seg + (piece + 1) * rows)
                fpad[group, place, :] = fbuf[piece, :, lanes].astype(jnp.float32)

    def convolve(targets, group, slot, lower=False):
        targets = [(jnp.maximum(lag, -1) * seg + 2 * seg, list(totals)) for lag, totals in targets]
        for shift in range(8):
            values = []
            for b in range(tiles):
                row = 8 * b + shift
                values.append(jnp.broadcast_to(mwork[slot, group, row : row + 1, :], (8, LANES)))
            for base, totals in targets:
                for gap in range(0 if lower else 1 - tiles, tiles):
                    window = fpad[group, pl.ds(base + (8 * gap - shift), 8), :]
                    for b in range(tiles):
                        if 0 <= b + gap < tiles:
                            totals[b + gap] = totals[b + gap] + window * values[b]
        return [totals for _, totals in targets]

    def zeros():
        return [jnp.zeros((8, LANES), jnp.float32) for _ in range(tiles)]

    def load_acc(half, group):
        return [acc[half, group, 8 * a : 8 * a + 8, :] for a in range(tiles)]

    def store_acc(half, group, totals):
        for a in range(tiles):
            acc[half, group, 8 * a : 8 * a + 8, :] = totals[a]

    count = 2 * n_seq

    def own_early(group, carry):
        (lead,) = convolve([(zero, zeros())], group, 0, lower=True)
        (tail,) = convolve([(count - 1 - 2 * early, zeros())], group, 0)
        store_acc(0, group, lead)
        store_acc(1, group, tail)
        return carry

    def own_late(group, carry):
        (tail,) = convolve([(zero, load_acc(1, group))], group, 1, lower=True)
        store_acc(1, group, tail)
        return carry

    def receive(half, ds):
        m_copies[half, ds].wait_recv()
        for group in range(groups):
            lanes = slice(group * LANES, (group + 1) * LANES)
            mwork[1 + ds, group] = mrecv[half, ds - 1, :, lanes].astype(jnp.float32)
        other = flip(seq, ds)
        return jnp.minimum(table_ref[2 * other], table_ref[2 * other + 1])

    def other_early(ds):
        theirs = receive(0, ds)

        def body(group, carry):
            lead, tail = convolve(
                [(early - theirs, load_acc(0, group)), (count - 1 - early - theirs, load_acc(1, group))],
                group,
                1 + ds,
            )
            store_acc(0, group, lead)
            store_acc(1, group, tail)
            return carry

        lax.fori_loop(0, groups, body, 0)

    def other_late(ds):
        theirs = receive(1, ds)

        def body(group, carry):
            (tail,) = convolve([(theirs - early, load_acc(1, group))], group, 1 + ds)
            store_acc(1, group, tail)
            return carry

        lax.fori_loop(0, groups, body, 0)

    order = list(range(n_z - 1, -1, -1))
    p_copies, s_copies = {}, {}
    relay = n_z == 4
    at_end = 1 - ((z + 1) // 2) % 2
    if relay:
        order = [3, 1, 2, 0]

    def for_partner():
        for group in range(groups):
            lanes = slice(group * LANES, (group + 1) * LANES)
            keep = in_order((seg, LANES))
            lead = acc[0, group]
            tail = acc[1, group]
            top = streams[0, 0:seg, lanes] * jnp.where(keep, lead, tail)
            bottom = streams[0, seg:rows, lanes] * jnp.where(keep, tail, lead)
            gated[0:seg, lanes] = top.astype(jnp.bfloat16)
            gated[seg:rows, lanes] = bottom.astype(jnp.bfloat16)
        for dz in order:
            columns = lanes_of(2 * flip(z, dz) + 1 - core)
            share = jnp.dot(gated[...], wout[:, columns], preferred_element_type=jnp.float32)
            psend[dz] = share.astype(jnp.bfloat16)
            p_copies[dz] = send(psend.at[dz], precv.at[dz], p_send.at[dz], p_recv.at[dz], chan=partner)

    def for_chips():
        for dz in order:
            share = jnp.dot(gated[...], wout[:, lanes_of(chan_of(dz))], preferred_element_type=jnp.float32)
            p_copies[dz].wait_recv()
            share = share + precv[dz].astype(jnp.float32)
            if dz == 0:
                share_own[...] = share
                continue
            target, slot = chan_of(dz), dz - 1
            if relay and dz == 3:
                target = 2 * ((1 - at_end) * flip(z, 3) + at_end * flip(z, 1)) + core
                slot = 2 + at_end
            if relay and dz == 2:

                @pl.when(at_end == 0)
                def _():
                    relayed().wait_recv()
                    ssend[1] = (share + srecv[3].astype(jnp.float32)).astype(jnp.bfloat16)

                @pl.when(at_end == 1)
                def _():
                    ssend[1] = share.astype(jnp.bfloat16)
            else:
                ssend[dz - 1] = share.astype(jnp.bfloat16)
            s_copies[dz] = send(
                ssend.at[dz - 1], srecv.at[slot], s_send.at[dz - 1], s_recv.at[slot], chan=target
            )

    def landing(slot):
        return pltpu.make_async_remote_copy(
            src_ref=ssend.at[0],
            dst_ref=srecv.at[slot],
            send_sem=s_send.at[0],
            recv_sem=s_recv.at[slot],
            device_id={"chan": partner},
            device_id_type=MESH,
        )

    def relayed():
        return landing(3)

    keys_values()
    own_table.wait()
    first = table_ref[2 * seq]
    second = table_ref[2 * seq + 1]
    early = jnp.minimum(first, second)
    zero = early * 0

    def in_order(shape):
        return jnp.full(shape, first) < jnp.full(shape, second)

    exchange()
    unpack_filters()
    lax.fori_loop(0, groups, own_early, 0)
    lax.fori_loop(0, groups, own_late, 0)
    queries()
    for ds in range(1, n_seq):
        other_early(ds)
    for ds in range(1, n_seq):
        other_late(ds)
    wout_copy.wait()
    for_partner()
    for_chips()
    if relay:

        @pl.when(at_end == 0)
        def _():
            landing(2).wait_recv()
            share_own[...] += srecv[2].astype(jnp.float32)

    total = share_own[...]
    for dz in range(1, 3 if relay else n_z):
        landing(dz - 1).wait_recv()
        total = total + srecv[dz - 1].astype(jnp.float32)
    out_ref[...] = total.astype(jnp.bfloat16)
    for copy in pending:
        copy.wait_send()


def on_device(n_seq, n_chan, hidden, filters, in_weight, out_weight, block_table):
    rows, chans = hidden.shape
    seg = rows // 2
    groups = chans // LANES
    n_z = n_chan // 2
    width = in_weight.shape[1]
    bf16, f32 = jnp.bfloat16, jnp.float32
    dma = pltpu.SemaphoreType.DMA
    in_hbm = pl.BlockSpec(memory_space=pltpu.HBM)
    return pl.pallas_call(
        functools.partial(kernel, n_seq, n_chan),
        out_shape=jax.ShapeDtypeStruct((rows, chans), bf16),
        in_specs=[in_hbm] * 5,
        out_specs=pl.BlockSpec(memory_space=pltpu.VMEM),
        scratch_shapes=[
            pltpu.SMEM(block_table.shape, jnp.int32),
            pltpu.VMEM((n_z, rows, 2 * chans), bf16),
            pltpu.VMEM((n_seq, rows, chans), bf16),
            pltpu.VMEM((3, width, chans), bf16),
            pltpu.VMEM((chans, width), bf16),
            pltpu.VMEM((3, rows, chans), f32),
            pltpu.VMEM((groups, 2 * seg + n_seq * rows, LANES), f32),
            pltpu.VMEM((2, seg, chans), bf16),
            pltpu.VMEM((2, n_seq - 1, seg, chans), bf16),
            pltpu.VMEM((n_seq + 1, groups, seg, LANES), f32),
            pltpu.VMEM((2, groups, seg, LANES), f32),
            pltpu.VMEM((rows, chans), bf16),
            pltpu.VMEM((n_z, rows, chans), bf16),
            pltpu.VMEM((n_z, rows, chans), bf16),
            pltpu.VMEM((n_z - 1, rows, chans), bf16),
            pltpu.VMEM((n_z, rows, chans), bf16),
            pltpu.VMEM((rows, chans), f32),
            dma((3,)),
            dma((2, n_z)),
            dma,
            dma((n_z - 1,)),
            dma((n_z - 1,)),
            dma((n_z,)),
            dma((n_z,)),
            dma((n_seq - 1,)),
            dma((n_seq - 1,)),
            dma((2, n_seq - 1)),
            dma((2, n_seq - 1)),
            dma((n_z,)),
            dma((n_z,)),
            dma((n_z - 1,)),
            dma((n_z,)),
        ],
        compiler_params=pltpu.CompilerParams(
            collective_id=0, has_side_effects=True, vmem_limit_bytes=64 * 1024 * 1024
        ),
        cost_estimate=pl.CostEstimate(
            flops=8 * rows * width * chans, bytes_accessed=8 * width * chans, transcendentals=0
        ),
    )(hidden, filters, in_weight, out_weight, block_table)


def solution(mesh):
    return jax.shard_map(
        functools.partial(on_device, mesh.shape["seq"], mesh.shape["chan"]),
        mesh=mesh,
        in_specs=(P("seq", "chan"), P("seq", "chan"), P(None, None, "chan"), P("chan", None), P()),
        out_specs=P("seq", "chan"),
        check_vma=False,
    )
```

```python
import functools

import jax
import jax.numpy as jnp
from jax import lax
from jax.experimental import pallas as pl
from jax.experimental.pallas import tpu as pltpu
from jax.sharding import PartitionSpec as P

MESH = pl.DeviceIdType.MESH
LANES = 128


def flip(value, bits):
    result, bit = value, 1
    while bit <= bits:
        if bits & bit:
            result = result + bit - 2 * bit * ((value // bit) % 2)
        bit *= 2
    return result


def kernel(
    n_seq,
    n_chan,
    hidden_ref,
    filters_ref,
    win_ref,
    wout_ref,
    table_hbm,
    out_ref,
    table_ref,
    hbuf,
    fbuf,
    win,
    wout,
    streams,
    fpad,
    msend,
    mrecv,
    mwork,
    acc,
    gated,
    psend,
    precv,
    ssend,
    srecv,
    share_own,
    own_sem,
    win_sem,
    wout_sem,
    hz_send,
    hz_recv,
    hp_send,
    hp_recv,
    f_send,
    f_recv,
    m_send,
    m_recv,
    p_send,
    p_recv,
    s_send,
    s_recv,
):
    rows, chans = hidden_ref.shape
    seg = rows // 2
    tiles = seg // 8
    groups = chans // LANES
    n_z = n_chan // 2
    seq = lax.axis_index("seq")
    chan = lax.axis_index("chan")
    z = chan // 2
    core = chan % 2
    partner = 2 * z + 1 - core

    def chan_of(dz):
        return 2 * flip(z, dz) + core

    def lanes_of(which):
        return pl.ds(pl.multiple_of(which * chans, chans), chans)

    pending = []

    def send(src, dst, send_sem, recv_sem, **where):
        copy = pltpu.make_async_remote_copy(
            src_ref=src,
            dst_ref=dst,
            send_sem=send_sem,
            recv_sem=recv_sem,
            device_id=where,
            device_id_type=MESH,
        )
        copy.start()
        pending.append(copy)
        return copy

    own_table = pltpu.make_async_copy(table_hbm, table_ref, own_sem.at[0])
    own_hidden = pltpu.make_async_copy(hidden_ref, hbuf.at[z, :, lanes_of(core)], own_sem.at[1])
    own_filters = pltpu.make_async_copy(filters_ref, fbuf.at[seq], own_sem.at[2])
    own_table.start()
    own_hidden.start()

    barrier = pltpu.get_barrier_semaphore()
    for ds in range(1, n_seq):
        pl.semaphore_signal(barrier, inc=1, device_id={"seq": flip(seq, ds)}, device_id_type=MESH)
    for dz in range(1, n_z):
        pl.semaphore_signal(barrier, inc=1, device_id={"chan": chan_of(dz)}, device_id_type=MESH)
    pl.semaphore_signal(barrier, inc=1, device_id={"chan": partner}, device_id_type=MESH)

    kv_copies, q_copies = [], []
    for dz in range(n_z):
        part = pl.ds(pl.multiple_of(flip(z, dz) * 2 * chans, 2 * chans), 2 * chans)
        kv_copies.append(
            pltpu.make_async_copy(win_ref.at[1:3, part, :], win.at[1:3, part, :], win_sem.at[0, dz])
        )
        q_copies.append(
            pltpu.make_async_copy(win_ref.at[0:1, part, :], win.at[0:1, part, :], win_sem.at[1, dz])
        )
    for copy in kv_copies:
        copy.start()
    own_filters.start()
    wout_copy = pltpu.make_async_copy(wout_ref, wout, wout_sem)

    pl.semaphore_wait(barrier, n_seq - 1 + n_z)

    to_chip, to_partner = {}, {}
    for dz in range(1, n_z):
        to_chip[dz] = send(
            hidden_ref, hbuf.at[z, :, lanes_of(core)], hz_send.at[dz - 1], hz_recv.at[dz - 1], chan=chan_of(dz)
        )
    to_partner[0] = send(hidden_ref, hbuf.at[z, :, lanes_of(core)], hp_send.at[0], hp_recv.at[0], chan=partner)
    filter_copies = [
        send(filters_ref, fbuf.at[seq], f_send.at[ds - 1], f_recv.at[ds - 1], seq=flip(seq, ds))
        for ds in range(1, n_seq)
    ]

    def project(dz, which, columns, add=True):
        chip = flip(z, dz)
        start = chip * 2 * chans + columns.start
        part = pl.ds(pl.multiple_of(start, chans), columns.size)
        total = jnp.dot(hbuf[chip, :, columns], win[which, part, :], preferred_element_type=jnp.float32)
        if add:
            total = streams[which] + total
        streams[which] = total

    m_copies = {}

    def keys_values():
        own_hidden.wait()
        for dz in range(n_z):
            if dz == n_z - 1:
                unpack_filters()
            if dz:
                to_chip[dz].wait_recv()
                spot = hbuf.at[flip(z, dz), :, lanes_of(core)]
                to_partner[dz] = send(spot, spot, hp_send.at[dz], hp_recv.at[dz], chan=partner)
            kv_copies[dz].wait()
            project(dz, 1, lanes_of(core), dz > 0)
            project(dz, 2, lanes_of(core), dz > 0)
            to_partner[dz].wait_recv()
            project(dz, 1, lanes_of(1 - core))
            project(dz, 2, lanes_of(1 - core))
            if dz == 0:
                for copy in q_copies:
                    copy.start()
            if dz == min(1, n_z - 1):
                wout_copy.start()

    def exchange():
        for half in range(2):
            for group in range(groups):
                lanes = slice(group * LANES, (group + 1) * LANES)
                product = streams[1, :, lanes] * streams[2, :, lanes]
                keep = in_order((seg, LANES))
                if half == 0:
                    product = jnp.where(keep, product[:seg], product[seg:])
                else:
                    product = jnp.where(keep, product[seg:], product[:seg])
                mwork[half, group] = product
                msend[half, :, lanes] = product.astype(jnp.bfloat16)
            for ds in range(1, n_seq):
                m_copies[half, ds] = send(
                    msend.at[half],
                    mrecv.at[half, ds - 1],
                    m_send.at[half, ds - 1],
                    m_recv.at[half, ds - 1],
                    seq=flip(seq, ds),
                )

    def queries():
        for dz in range(n_z):
            project(dz, 0, pl.ds(0, 2 * chans), dz > 0)

    def unpack_filters():
        own_filters.wait()
        for copy in filter_copies:
            copy.wait_recv()
        for group in range(groups):
            lanes = slice(group * LANES, (group + 1) * LANES)
            fpad[group, 0 : 2 * seg, :] = jnp.zeros((2 * seg, LANES), jnp.float32)
            for piece in range(n_seq):
                place = slice(2 * seg + piece * rows, 2 * seg + (piece + 1) * rows)
                fpad[group, place, :] = fbuf[piece, :, lanes].astype(jnp.float32)

    def convolve(targets, group, slot, lower=False):
        targets = [(jnp.maximum(lag, -1) * seg + 2 * seg, list(totals)) for lag, totals in targets]
        for shift in range(8):
            values = []
            for b in range(tiles):
                row = 8 * b + shift
                values.append(jnp.broadcast_to(mwork[slot, group, row : row + 1, :], (8, LANES)))
            for base, totals in targets:
                for gap in range(0 if lower else 1 - tiles, tiles):
                    window = fpad[group, pl.ds(base + (8 * gap - shift), 8), :]
                    for b in range(tiles):
                        if 0 <= b + gap < tiles:
                            totals[b + gap] = totals[b + gap] + window * values[b]
        return [totals for _, totals in targets]

    def zeros():
        return [jnp.zeros((8, LANES), jnp.float32) for _ in range(tiles)]

    def load_acc(half, group):
        return [acc[half, group, 8 * a : 8 * a + 8, :] for a in range(tiles)]

    def store_acc(half, group, totals):
        for a in range(tiles):
            acc[half, group, 8 * a : 8 * a + 8, :] = totals[a]

    def for_groups(body):
        for group in range(groups):
            body(group, 0)

    count = 2 * n_seq

    def own_early(group, carry):
        (lead,) = convolve([(zero, zeros())], group, 0, lower=True)
        (tail,) = convolve([(count - 1 - 2 * early, zeros())], group, 0)
        store_acc(0, group, lead)
        store_acc(1, group, tail)
        return carry

    def own_late(group, carry):
        (tail,) = convolve([(zero, load_acc(1, group))], group, 1, lower=True)
        store_acc(1, group, tail)
        return carry

    def receive(half, ds):
        m_copies[half, ds].wait_recv()
        for group in range(groups):
            lanes = slice(group * LANES, (group + 1) * LANES)
            mwork[1 + ds, group] = mrecv[half, ds - 1, :, lanes].astype(jnp.float32)
        other = flip(seq, ds)
        return jnp.minimum(table_ref[2 * other], table_ref[2 * other + 1])

    def other_early(ds):
        theirs = receive(0, ds)

        def body(group, carry):
            lead, tail = convolve(
                [(early - theirs, load_acc(0, group)), (count - 1 - early - theirs, load_acc(1, group))],
                group,
                1 + ds,
            )
            store_acc(0, group, lead)
            store_acc(1, group, tail)
            return carry

        for_groups(body)

    def other_late(ds):
        theirs = receive(1, ds)

        def body(group, carry):
            (tail,) = convolve([(theirs - early, load_acc(1, group))], group, 1 + ds)
            store_acc(1, group, tail)
            return carry

        for_groups(body)

    order = list(range(n_z - 1, -1, -1))
    p_copies, s_copies = {}, {}
    relay = n_z == 4
    at_end = 1 - ((z + 1) // 2) % 2
    if relay:
        order = [3, 1, 2, 0]

    def for_partner():
        for group in range(groups):
            lanes = slice(group * LANES, (group + 1) * LANES)
            keep = in_order((seg, LANES))
            lead = acc[0, group]
            tail = acc[1, group]
            top = streams[0, 0:seg, lanes] * jnp.where(keep, lead, tail)
            bottom = streams[0, seg:rows, lanes] * jnp.where(keep, tail, lead)
            gated[0:seg, lanes] = top.astype(jnp.bfloat16)
            gated[seg:rows, lanes] = bottom.astype(jnp.bfloat16)
        for dz in order:
            columns = lanes_of(2 * flip(z, dz) + 1 - core)
            share = jnp.dot(gated[...], wout[:, columns], preferred_element_type=jnp.float32)
            psend[dz] = share.astype(jnp.bfloat16)
            p_copies[dz] = send(psend.at[dz], precv.at[dz], p_send.at[dz], p_recv.at[dz], chan=partner)

    def for_chips():
        for dz in order:
            share = jnp.dot(gated[...], wout[:, lanes_of(chan_of(dz))], preferred_element_type=jnp.float32)
            p_copies[dz].wait_recv()
            share = share + precv[dz].astype(jnp.float32)
            if dz == 0:
                share_own[...] = share
                continue
            target, slot = chan_of(dz), dz - 1
            if relay and dz == 3:
                target = 2 * ((1 - at_end) * flip(z, 3) + at_end * flip(z, 1)) + core
                slot = 2 + at_end
            if relay and dz == 2:

                @pl.when(at_end == 0)
                def _():
                    relayed().wait_recv()
                    ssend[1] = (share + srecv[3].astype(jnp.float32)).astype(jnp.bfloat16)

                @pl.when(at_end == 1)
                def _():
                    ssend[1] = share.astype(jnp.bfloat16)
            else:
                ssend[dz - 1] = share.astype(jnp.bfloat16)
            s_copies[dz] = send(
                ssend.at[dz - 1], srecv.at[slot], s_send.at[dz - 1], s_recv.at[slot], chan=target
            )

    def landing(slot):
        return pltpu.make_async_remote_copy(
            src_ref=ssend.at[0],
            dst_ref=srecv.at[slot],
            send_sem=s_send.at[0],
            recv_sem=s_recv.at[slot],
            device_id={"chan": partner},
            device_id_type=MESH,
        )

    def relayed():
        return landing(3)

    keys_values()
    own_table.wait()
    first = table_ref[2 * seq]
    second = table_ref[2 * seq + 1]
    early = jnp.minimum(first, second)
    zero = early * 0

    def in_order(shape):
        return jnp.full(shape, first) < jnp.full(shape, second)

    exchange()
    for copy in q_copies:
        copy.wait()
    for_groups(own_early)
    queries()
    for_groups(own_late)
    for ds in range(1, n_seq):
        other_early(ds)
    for ds in range(1, n_seq):
        other_late(ds)
    wout_copy.wait()
    for_partner()
    for_chips()
    if relay:

        @pl.when(at_end == 0)
        def _():
            landing(2).wait_recv()
            share_own[...] += srecv[2].astype(jnp.float32)

    total = share_own[...]
    for dz in range(1, 3 if relay else n_z):
        landing(dz - 1).wait_recv()
        total = total + srecv[dz - 1].astype(jnp.float32)
    out_ref[...] = total.astype(jnp.bfloat16)
    for copy in pending:
        copy.wait_send()


def on_device(n_seq, n_chan, hidden, filters, in_weight, out_weight, block_table):
    rows, chans = hidden.shape
    seg = rows // 2
    groups = chans // LANES
    n_z = n_chan // 2
    width = in_weight.shape[1]
    bf16, f32 = jnp.bfloat16, jnp.float32
    dma = pltpu.SemaphoreType.DMA
    in_hbm = pl.BlockSpec(memory_space=pltpu.HBM)
    return pl.pallas_call(
        functools.partial(kernel, n_seq, n_chan),
        out_shape=jax.ShapeDtypeStruct((rows, chans), bf16),
        in_specs=[in_hbm] * 5,
        out_specs=pl.BlockSpec(memory_space=pltpu.VMEM),
        scratch_shapes=[
            pltpu.SMEM(block_table.shape, jnp.int32),
            pltpu.VMEM((n_z, rows, 2 * chans), bf16),
            pltpu.VMEM((n_seq, rows, chans), bf16),
            pltpu.VMEM((3, width, chans), bf16),
            pltpu.VMEM((chans, width), bf16),
            pltpu.VMEM((3, rows, chans), f32),
            pltpu.VMEM((groups, 2 * seg + n_seq * rows, LANES), f32),
            pltpu.VMEM((2, seg, chans), bf16),
            pltpu.VMEM((2, n_seq - 1, seg, chans), bf16),
            pltpu.VMEM((n_seq + 1, groups, seg, LANES), f32),
            pltpu.VMEM((2, groups, seg, LANES), f32),
            pltpu.VMEM((rows, chans), bf16),
            pltpu.VMEM((n_z, rows, chans), bf16),
            pltpu.VMEM((n_z, rows, chans), bf16),
            pltpu.VMEM((n_z - 1, rows, chans), bf16),
            pltpu.VMEM((n_z, rows, chans), bf16),
            pltpu.VMEM((rows, chans), f32),
            dma((3,)),
            dma((2, n_z)),
            dma,
            dma((n_z - 1,)),
            dma((n_z - 1,)),
            dma((n_z,)),
            dma((n_z,)),
            dma((n_seq - 1,)),
            dma((n_seq - 1,)),
            dma((2, n_seq - 1)),
            dma((2, n_seq - 1)),
            dma((n_z,)),
            dma((n_z,)),
            dma((n_z - 1,)),
            dma((n_z,)),
        ],
        compiler_params=pltpu.CompilerParams(
            collective_id=0, has_side_effects=True, vmem_limit_bytes=64 * 1024 * 1024
        ),
        cost_estimate=pl.CostEstimate(
            flops=8 * rows * width * chans, bytes_accessed=8 * width * chans, transcendentals=0
        ),
    )(hidden, filters, in_weight, out_weight, block_table)


def solution(mesh):
    return jax.shard_map(
        functools.partial(on_device, mesh.shape["seq"], mesh.shape["chan"]),
        mesh=mesh,
        in_specs=(P("seq", "chan"), P("seq", "chan"), P(None, None, "chan"), P("chan", None), P()),
        out_specs=P("seq", "chan"),
        check_vma=False,
    )
```
